32 devices in a mesh: groups: 2 (over y), tensor: 4 (over x, core), job: 4 (over z).
Axes of the slice: x: 2, y: 2, z: 4, core: 2. Of those that a mesh axis runs over, the one named last changes fastest.
Arguments:
- inputs: bfloat16 [8, 1024, 12288], P(('groups', 'job'), None, 'tensor'), parts along dimension 0, may hold values from -6 to 6
- grad_out: bfloat16 [8, 1024, 1024], P(('groups', 'job'), 'tensor'), parts along dimension 0, may hold values from -6 to 6
- value_weight: bfloat16 [12288, 1024], P('tensor'), may hold values from -0.1875 to 0.1875
- adapter_down: bfloat16 [8, 12288, 128], P(('groups', 'job'), 'tensor'), parts along dimension 0, may hold values from -0.25 to 0.25
- adapter_up: bfloat16 [8, 1024, 128], P(('groups', 'job'), 'tensor'), parts along dimension 0, may hold values from -0.1875 to 0.1875
- block_adapter: int32 [8, 8], P(('groups', 'job')), parts along dimension 0, may hold values from 0 to 3
- block_length: int32 [8, 8], P(('groups', 'job')), parts along dimension 0, may hold values from 1 to 128
- owner_slot: int32 [8], P('groups'), parts along dimension 0, may hold values from 0 to 3, as said below
- adapter_rank: int32 [8], P('groups'), parts along dimension 0, may hold values from 16 to 128, as said below
Outputs:
- grad_in: bfloat16 [8, 1024, 12288], P(('groups', 'job'), None, 'tensor'), parts along dimension 0
- grad_down: float32 [8, 12288, 128], P(('groups', 'job'), 'tensor'), parts along dimension 0
- grad_up: float32 [8, 1024, 128], P(('groups', 'job'), 'tensor'), parts along dimension 0
The draws below stay inside these ranges and needn't reach their ends.
There are 2 independent parts, one for each index of `groups`. The reference program is written for one: setup_inputs(seed, part) draws one part's arguments, and reference() takes and returns one part's arrays. A program takes and returns all parts, laid end to end along the dimension named above; an argument that names none is the same for every part. Nothing has to cross between parts.
Inputs may be any that keep to these rules, and one draw needn't show every extreme that they name: `owner_slot`: each slot owns exactly one adapter. `adapter_rank`: every rank is 128, 64, 32 or 16, each for a quarter of the adapters.
All inputs are finite; a program needn't handle non-finite values.
Results may differ from the reference program's by a relative error of at most 0.015.
Values may be sent and summed in bfloat16 or wider, within the bound.
No kernel may reach another device: no remote copies, remote signals or barrier semaphores. Data moves between devices by JAX's collectives and lax.ppermute only.
A program may use at most 128 MiB of HBM per device.

```python
import math
import jax
import jax.numpy as jnp
import numpy as np
from jax import lax

D = 12288
KV = 1024
R = 128
BLOCK = 128
BLOCKS = 8
ROWS = 1024
BATCHES = 4
ADAPTERS = 4


def draw_owner_slot(key, part):
    key = jax.random.fold_in(key, 11)
    return jax.random.permutation(key, jnp.arange(ADAPTERS, dtype=jnp.int32)).astype(jnp.int32)


def draw_adapter_rank(key, part):
    key = jax.random.fold_in(key, 7)
    shuffled = jax.random.permutation(key, ADAPTERS)
    halvings = jnp.remainder(shuffled, 4).astype(jnp.int32)
    return (R // jnp.left_shift(jnp.int32(1), halvings)).astype(jnp.int32)


def set_ends(result, rng, least, largest):
    longest = result.shape.index(max(result.shape))
    spots = []
    for shift in (0, 1):
        where = [jax.random.randint(jax.random.fold_in(rng, axis), (), 0, length) for axis, length in enumerate(result.shape)]
        where[longest] = (where[longest] + shift) % result.shape[longest]
        spots.append(tuple(where))
    return result.at[spots[0]].set(least).at[spots[1]].set(largest)


def shard_levels(stream_key, shape, shards, least, top_value):
    loudness, own = 1.0, jax.random.fold_in(stream_key, 6)
    for axis_at, shards_of in shards:
        steps = jnp.exp(jax.random.uniform(jax.random.fold_in(own, axis_at), (shards_of,), jnp.float32, least / len(shards), top_value / len(shards)))
        loudness = loudness * jnp.repeat(steps, shape[axis_at] // shards_of).reshape([-1 if axis == axis_at else 1 for axis in range(len(shape))])
    return loudness


def rank_table(count, slope):
    loads = [(1 << 20) // math.isqrt(rank ** slope) + 1 for rank in range(1, count + 1)]
    scale = 1 + sum(loads) // (1 << 30)
    return np.cumsum(np.array([max(1, weight // scale) for weight in loads]))


def ranked_ids(own_key, shape, number_of, skew):
    grid = rank_table(number_of, skew)
    pick = jax.random.randint(jax.random.fold_in(own_key, 1), shape, 0, int(grid[number_of - 1]))
    standing = jnp.searchsorted(jnp.asarray(grid, jnp.int32), pick, side="right")
    return jax.random.permutation(jax.random.fold_in(own_key, 2), number_of)[standing].astype(jnp.int32)


def gaussian(own_key, dims, spread, limit, shards=(), kind=jnp.bfloat16):
    values = spread * jax.random.normal(own_key, dims, jnp.float32)
    if shards:
        values = values * shard_levels(own_key, dims, shards, -0.22, 0.18)
    return jnp.clip(values, -limit, limit).astype(kind)


def setup_inputs(seed: int = 0, part: int = 0) -> dict:
    seeds = jax.random.split(jax.random.key(seed), 10)
    own_keys = jax.random.split(jax.random.fold_in(seeds[9], part), 10)
    return {
        "inputs": gaussian(own_keys[0], (BATCHES, ROWS, D), 1.0, 6.0, ((0, 4), (2, 4))),
        "grad_out": gaussian(own_keys[1], (BATCHES, ROWS, KV), 1.0, 6.0, ((0, 4), (1, 4))),
        "value_weight": gaussian(seeds[2], (D, KV), KV ** -0.5, 0.1875, ((0, 4),)),
        "adapter_down": gaussian(own_keys[3], (ADAPTERS, D, R), (4 * R) ** -0.5, 0.25, ((0, 4), (1, 4))),
        "adapter_up": gaussian(own_keys[4], (ADAPTERS, KV, R), KV ** -0.5, 0.1875, ((0, 4), (1, 4))),
        "block_adapter": set_ends(ranked_ids(own_keys[5], (BATCHES, BLOCKS), ADAPTERS, 2), jax.random.fold_in(own_keys[5], 3), 0, ADAPTERS - 1).astype(jnp.int32),
        "block_length": set_ends(jax.random.randint(own_keys[6], (BATCHES, BLOCKS), 1, BLOCK + 1), jax.random.fold_in(own_keys[6], 1), 1, BLOCK).astype(jnp.int32),
        "owner_slot": draw_owner_slot(jax.random.fold_in(jax.random.fold_in(seeds[9], part), 71), part),
        "adapter_rank": draw_adapter_rank(jax.random.fold_in(jax.random.fold_in(seeds[9], part), 71), part),
    }


def block_tables(block_ids, block_sizes, owner_slot, adapter_rank, block_rows, rank_width):
    adapter_count = owner_slot.shape[0]
    matches = (block_ids[:, None] == jnp.arange(adapter_count, dtype=jnp.int32)[None, :]).astype(jnp.int32)
    slot_index = lax.optimization_barrier(jnp.sum(matches * owner_slot[None, :], axis=1)).astype(jnp.int32)
    rank_used = lax.optimization_barrier(jnp.sum(matches * adapter_rank[None, :], axis=1)).astype(jnp.int32)
    selector = (slot_index[:, None] == jnp.arange(adapter_count, dtype=jnp.int32)[None, :]).astype(jnp.float32)
    live_rows = (jnp.arange(block_rows, dtype=jnp.int32)[None, :] < block_sizes[:, None]).astype(jnp.float32)
    keep_ranks = (jnp.arange(rank_width, dtype=jnp.int32)[None, :] < rank_used[:, None]).astype(jnp.float32)
    scaling = rank_width / (2.0 * rank_used.astype(jnp.float32))
    factor = live_rows[:, :, None] * keep_ranks[:, None, :] * scaling[:, None, None]
    return (slot_index, selector, live_rows, factor)

def reference(inputs, grad_out, value_weight, adapter_down, adapter_up, block_adapter, block_length, owner_slot, adapter_rank):
    highest = lax.Precision.HIGHEST
    scaling_norm = 1.0 / math.sqrt(BATCHES * ROWS)

    def one_batch(carry, items):
        total_down, total_up = carry
        features, cotangent, block_ids, block_sizes = items
        slot_index, selector, live_rows, factor = block_tables(block_ids, block_sizes, owner_slot, adapter_rank, BLOCK, R)
        down_used = jnp.take(adapter_down, slot_index, axis=0).astype(jnp.float32)
        up_used = jnp.take(adapter_up, slot_index, axis=0).astype(jnp.float32)
        feat_blocks = features.reshape(BLOCKS, BLOCK, D).astype(jnp.float32)
        cot_blocks = cotangent.reshape(BLOCKS, BLOCK, KV).astype(jnp.float32)
        projected = jnp.einsum('btd,bdr->btr', feat_blocks, down_used, precision=highest)
        pulled = jnp.einsum('btk,bkr->btr', cot_blocks, up_used, precision=highest)
        low_down = (projected * factor).astype(jnp.bfloat16)
        low_grad = (pulled * factor).astype(jnp.bfloat16)
        base_term = jnp.dot(cotangent, value_weight.T, preferred_element_type=jnp.float32)
        adapter_term = jnp.einsum('btr,bdr->btd', low_grad.astype(jnp.float32), down_used, precision=highest).reshape(ROWS, D)
        grad_rows = (base_term * live_rows.reshape(ROWS)[:, None] + adapter_term).astype(jnp.bfloat16)
        block_down = jnp.einsum('btd,btr->bdr', feat_blocks, low_grad.astype(jnp.float32), precision=highest)
        block_up = jnp.einsum('btk,btr->bkr', cot_blocks, low_down.astype(jnp.float32), precision=highest)
        part_down = (jnp.einsum('bs,bdr->sdr', selector, block_down, precision=highest) * scaling_norm).astype(jnp.bfloat16)
        part_up = (jnp.einsum('bs,bkr->skr', selector, block_up, precision=highest) * scaling_norm).astype(jnp.bfloat16)
        return ((total_down + part_down.astype(jnp.float32), total_up + part_up.astype(jnp.float32)), grad_rows)
    adapter_count = owner_slot.shape[0]
    empty_down = jnp.zeros((adapter_count, D, R), jnp.float32)
    empty_up = jnp.zeros((adapter_count, KV, R), jnp.float32)
    (grad_down, grad_up), grad_in = lax.scan(one_batch, (empty_down, empty_up), (inputs, grad_out, block_adapter, block_length))
    return (grad_in, grad_down, grad_up)
```

```python
import functools
import math

import jax
import jax.numpy as jnp
from jax import lax
from jax.experimental import pallas as pl
from jax.experimental.pallas import tpu as pltpu
from jax.sharding import PartitionSpec as P

F32 = jnp.float32
BF16 = jnp.bfloat16
VMEM_LIMIT = 40 * 1024 * 1024
CHUNKS = 5
JOBS = 4
PAIR = [(0, 1), (1, 0), (2, 3), (3, 2)]
MIDDLE = [(1, 2), (2, 1)]
TENSOR_X = [(0, 2), (2, 0), (1, 3), (3, 1)]
TENSOR_CORE = [(0, 1), (1, 0), (2, 3), (3, 2)]


def params():
    return pltpu.CompilerParams(vmem_limit_bytes=VMEM_LIMIT)


def cost(flops, moved):
    return pl.CostEstimate(flops=flops, bytes_accessed=moved, transcendentals=0)


def whole(shape):
    return pl.BlockSpec(shape, lambda *_: (0,) * len(shape))


def smem():
    return pl.BlockSpec(memory_space=pltpu.SMEM)


def turn_kernel(down_ref, low_ref, high_ref):
    turned = down_ref[...].T
    half = low_ref.shape[0]
    low_ref[...] = turned[:half]
    high_ref[...] = turned[half:]


def turn(down, tile):
    width, rank = down.shape
    half = rank // 2
    out = jax.ShapeDtypeStruct((half, width), down.dtype)
    return pl.pallas_call(
        turn_kernel,
        grid=(width // tile,),
        in_specs=[pl.BlockSpec((tile, rank), lambda i: (i, 0))],
        out_specs=[pl.BlockSpec((half, tile), lambda i: (0, i))] * 2,
        out_shape=[out, out],
        compiler_params=params(),
        cost_estimate=cost(0, 4 * width * rank),
        name="turn_adapter",
    )(down)


def block_factor(ids, lengths, owners, ranks, b, rows, width):
    adapter = ids[0, b]
    rank = ranks[adapter]
    live = lax.broadcasted_iota(jnp.int32, (rows, width), 0) < lengths[0, b]
    keep = lax.broadcasted_iota(jnp.int32, (rows, width), 1) < rank
    scale = jnp.float32(width) / (2.0 * rank.astype(F32))
    return owners[adapter], jnp.where(live & keep, scale, 0.0)


def spread(low, slot):
    half = low.shape[1] // 2
    lanes = lax.broadcasted_iota(jnp.int32, low.shape, 1)
    turned = pltpu.roll(low, half, 1)
    twice = jnp.where(lanes < half, low, turned)
    chunk = jnp.where(lanes < half, 0, 1)
    return jnp.concatenate(
        [
            jnp.where(chunk == slot, twice, 0.0),
            jnp.where(chunk + 2 == slot, twice, 0.0),
            jnp.where(lanes < half, turned, 0.0),
        ],
        axis=1,
    )


def gathered(full, slot, rank):
    half = rank // 2
    odd = lax.rem(slot, 2)
    both = jnp.where(slot >= 2, full[:, rank : 2 * rank], full[:, :rank])
    turned = pltpu.roll(both, half, 1)
    lower = jnp.where(odd == 1, turned, both)
    upper = pltpu.roll(full[:, 2 * rank :], half, 1)
    lanes = lax.broadcasted_iota(jnp.int32, both.shape, 1)
    return jnp.where(lanes < half, lower, upper)


def pull_kernel(norm, ids, lengths, owners, ranks, place, g0, g1, g2, g3, u0, u1, u2, u3, x_ref,
                part_ref, wide_ref, up, turned):
    t, z = place[0], place[1]
    quarter, values = g0.shape
    rank = u0.shape[2]
    block = x_ref.shape[0] // ids.shape[1]

    @pl.when(pl.program_id(0) == 0)
    def _():
        for q, u in enumerate((u0, u1, u2, u3)):
            start = pl.multiple_of(jnp.bitwise_xor(t, q) * quarter, quarter)
            for d in range(JOBS):
                slot = lax.rem(z - d + JOBS, JOBS)
                up[slot, pl.ds(start, quarter), :] = u[d]
        for q, g in enumerate((g0, g1, g2, g3)):
            for j in range(quarter // block):
                b = jnp.bitwise_xor(t, q) * (quarter // block) + j
                slot, factor = block_factor(ids, lengths, owners, ranks, b, block, rank)
                pulled = jnp.dot(g[j * block : (j + 1) * block, :], up[slot], preferred_element_type=F32)
                low = spread((pulled * factor).astype(BF16).astype(F32), slot)
                rows = pl.ds(pl.multiple_of(b * block, block), block)
                wide_ref[rows, :] = low.astype(BF16)
                turned[:, rows] = low.T.astype(BF16)

    used = part_ref.shape[0]
    part_ref[...] = (
        jnp.dot(turned[:used, :], x_ref[...], preferred_element_type=F32) * norm
    ).astype(BF16)


def pull(tables, place, grads, ups, features, norm, tile):
    rows, width = features.shape
    quarter, values = grads[0].shape
    rank = ups[0].shape[2]
    used = CHUNKS * rank // 2
    return pl.pallas_call(
        functools.partial(pull_kernel, norm),
        grid=(width // tile,),
        in_specs=[smem()] * 5
        + [whole((quarter, values))] * 4
        + [whole((JOBS, quarter, rank))] * 4
        + [pl.BlockSpec((rows, tile), lambda i: (0, i))],
        out_specs=[
            pl.BlockSpec((used, tile), lambda i: (0, i)),
            whole((rows, 3 * rank)),
        ],
        out_shape=[
            jax.ShapeDtypeStruct((used, width), BF16),
            jax.ShapeDtypeStruct((rows, 3 * rank), BF16),
        ],
        scratch_shapes=[
            pltpu.VMEM((JOBS, values, rank), BF16),
            pltpu.VMEM((3 * rank, rows), BF16),
        ],
        compiler_params=params(),
        cost_estimate=cost(2 * used * rows * width, 2 * (rows * width + used * width + 2 * rows * values)),
        name="pull_and_part_down",
    )(*tables, place, *grads, *ups, features)


def project_kernel(ids, owners, where_to, *refs):
    chunks = refs[:9]
    x_ref, out_ref, table_ref, sems = refs[9:]
    half, width = chunks[0].shape
    rank = 2 * half
    rows = x_ref.shape[0]
    block = rank

    @pl.when(pl.program_id(0) == 0)
    def _():
        for k, chunk in enumerate(chunks):
            place = where_to[k]

            @pl.when(place < CHUNKS)
            def _():
                start = pl.multiple_of(place * half, half)
                pltpu.make_async_copy(chunk, table_ref.at[pl.ds(start, half), :], sems.at[k]).start()

        table_ref[CHUNKS * half :, :] = jnp.zeros((half, width), BF16)
        for k, chunk in enumerate(chunks):
            place = where_to[k]

            @pl.when(place < CHUNKS)
            def _():
                start = pl.multiple_of(place * half, half)
                pltpu.make_async_copy(chunk, table_ref.at[pl.ds(start, half), :], sems.at[k]).wait()

    full = lax.dot_general(
        x_ref[...], table_ref[...], (((1,), (1,)), ((), ())), preferred_element_type=F32
    )
    first = pl.program_id(0) * (rows // block)
    for j in range(rows // block):
        slot = owners[ids[0, first + j]]
        piece = gathered(full[j * block : (j + 1) * block], slot, rank)
        out_ref[j * block : (j + 1) * block, :] = piece.astype(BF16)


def project(ids, owners, where_to, chunks, features, tile):
    rows, width = features.shape
    half = chunks[0].shape[0]
    return pl.pallas_call(
        project_kernel,
        grid=(rows // tile,),
        in_specs=[smem()] * 3
        + [pl.BlockSpec(memory_space=pl.ANY)] * 9
        + [pl.BlockSpec((tile, width), lambda i: (i, 0))],
        out_specs=[
            pl.BlockSpec((tile, 2 * half), lambda i: (i, 0)),
            whole((6 * half, width)),
        ],
        out_shape=[
            jax.ShapeDtypeStruct((rows, 2 * half), BF16),
            jax.ShapeDtypeStruct((6 * half, width), BF16),
        ],
        scratch_shapes=[pltpu.SemaphoreType.DMA((9,))],
        compiler_params=params(),
        cost_estimate=cost(2 * 6 * half * rows * width, 2 * (rows * width + 12 * half * width)),
        name="project",
    )(ids, owners, where_to, *chunks, features)


def base_kernel(lengths, place, g0, g1, g2, g3, wide_ref, weight_ref, table_ref, out_ref):
    t = place[0]
    quarter, values = g0.shape
    block = out_ref.shape[0] // lengths.shape[1]
    tile = out_ref.shape[1]
    for q, g in enumerate((g0, g1, g2, g3)):
        start = pl.multiple_of(jnp.bitwise_xor(t, q) * quarter, quarter)
        base = lax.dot_general(
            g[...], weight_ref[...], (((1,), (1,)), ((), ())), preferred_element_type=F32
        )
        term = jnp.dot(wide_ref[pl.ds(start, quarter), :], table_ref[...], preferred_element_type=F32)
        for j in range(quarter // block):
            b = jnp.bitwise_xor(t, q) * (quarter // block) + j
            live = lax.broadcasted_iota(jnp.int32, (block, tile), 0) < lengths[0, b]
            part = slice(j * block, (j + 1) * block)
            out_ref[pl.ds(pl.multiple_of(start + j * block, block), block), :] = (
                jnp.where(live, base[part], 0.0) + term[part]
            ).astype(BF16)


def base(lengths, place, grads, wide, weight, table, tile):
    width, values = weight.shape
    quarter = grads[0].shape[0]
    rows, deep = wide.shape
    return pl.pallas_call(
        base_kernel,
        grid=(width // tile,),
        in_specs=[smem()] * 2
        + [whole((quarter, values))] * 4
        + [
            whole((rows, deep)),
            pl.BlockSpec((tile, values), lambda i: (i, 0)),
            pl.BlockSpec((deep, tile), lambda i: (0, i)),
        ],
        out_specs=pl.BlockSpec((rows, tile), lambda i: (0, i)),
        out_shape=jax.ShapeDtypeStruct((rows, width), BF16),
        compiler_params=params(),
        cost_estimate=cost(
            2 * rows * width * (values + deep), 2 * (rows * values + width * values + deep * width + rows * width)
        ),
        name="grad_rows",
    )(lengths, place, *grads, wide, weight, table)


def part_up_kernel(norm, ids, lengths, owners, ranks, place, g0, g1, g2, g3, a_ref, b_ref, *rest):
    outs, (slice_ref, wide) = rest[:JOBS], rest[JOBS:]
    t, z, excess = place[0], place[1], place[2]
    quarter, values = g0.shape
    rank = a_ref.shape[1]
    half = rank // 2
    block = a_ref.shape[0] // ids.shape[1]
    columns = pl.ds(pl.multiple_of(t * quarter, quarter), quarter)
    for q, g in enumerate((g0, g1, g2, g3)):
        start = pl.multiple_of(jnp.bitwise_xor(t, q) * quarter, quarter)
        slice_ref[pl.ds(start, quarter), :] = g[:, columns]
    for b in range(ids.shape[1]):
        slot, factor = block_factor(ids, lengths, owners, ranks, b, block, rank)
        rows = slice(b * block, (b + 1) * block)
        low = (a_ref[rows, :].astype(F32) + b_ref[rows, :].astype(F32)) * factor
        wide[rows, :] = spread(low.astype(BF16).astype(F32), slot).astype(BF16)
    full = (
        lax.dot_general(slice_ref[...], wide[...], (((0,), (0,)), ((), ())), preferred_element_type=F32) * norm
    )
    lanes = lax.broadcasted_iota(jnp.int32, (quarter, rank), 1)
    for d, out in enumerate(outs):
        slot = lax.rem(z + d, JOBS)
        keep = jnp.where(slot == excess, rank, half)
        out[...] = jnp.where(lanes < keep, gathered(full, slot, rank), 0.0).astype(BF16)


def part_up(tables, place, grads, sums, norm):
    quarter, values = grads[0].shape
    rows, rank = sums[0].shape
    vmem = pl.BlockSpec(memory_space=pltpu.VMEM)
    return pl.pallas_call(
        functools.partial(part_up_kernel, norm),
        in_specs=[smem()] * 5 + [vmem] * 6,
        out_specs=[vmem] * JOBS,
        out_shape=[jax.ShapeDtypeStruct((quarter, rank), BF16)] * JOBS,
        scratch_shapes=[
            pltpu.VMEM((rows, quarter), BF16),
            pltpu.VMEM((rows, 3 * rank), BF16),
        ],
        compiler_params=params(),
        cost_estimate=cost(2 * rows * quarter * 3 * rank, 2 * (rows * values + 2 * rows * rank)),
        name="part_up",
    )(*tables, place, *grads, *sums)


def last_kernel(place, own0, own1, t1, n1, t2, n2, out_ref):
    half = own0.shape[0]
    rank = 2 * half
    total = (
        jnp.concatenate([own0[...], own1[...]], axis=0).astype(F32)
        + jnp.concatenate([t1[...], t2[...]], axis=0).astype(F32)
        + jnp.concatenate([n1[...], n2[...]], axis=0).astype(F32)
    )
    keep = jnp.where(place[1] == place[2], rank, half)
    rows = lax.broadcasted_iota(jnp.int32, total.shape, 0)
    out_ref[...] = jnp.where(rows < keep, total, 0.0).T


def last(place, parts, t1, n1, t2, n2, tile):
    half, width = t1.shape
    piece = pl.BlockSpec((half, tile), lambda i, place: (0, i))
    return pl.pallas_call(
        last_kernel,
        grid_spec=pltpu.PrefetchScalarGridSpec(
            num_scalar_prefetch=1,
            grid=(width // tile,),
            in_specs=[
                pl.BlockSpec((half, tile), lambda i, place: (place[1], i)),
                pl.BlockSpec((half, tile), lambda i, place: (CHUNKS - 1, i)),
            ]
            + [piece] * 4,
            out_specs=pl.BlockSpec((tile, 2 * half), lambda i, place: (i, 0)),
        ),
        out_shape=jax.ShapeDtypeStruct((width, 2 * half), F32),
        compiler_params=params(),
        cost_estimate=cost(0, 2 * 6 * half * width + 8 * half * width),
        name="grad_down",
    )(place, parts, parts, t1, n1, t2, n2)


def on_device(
    inputs,
    grad_out,
    value_weight,
    adapter_down,
    adapter_up,
    block_adapter,
    block_length,
    owner_slot,
    adapter_rank,
):
    features = inputs[0]
    row_count, local_width = features.shape
    half = adapter_down.shape[2] // 2
    tile = 512
    norm = 1.0 / math.sqrt(JOBS * row_count)
    t, z = lax.axis_index("tensor"), lax.axis_index("job")
    excess = jnp.sum(jnp.where(adapter_rank > half, owner_slot, 0)).astype(jnp.int32)
    place = jnp.stack([t, z, excess]).astype(jnp.int32)
    tables = (block_adapter, block_length, owner_slot, adapter_rank)

    inner = (z == 1) | (z == 2)
    mine = jnp.where(z < 2, 1, 2)
    outer = jnp.where(z < 2, 0, 3)
    far_in, far_out = 3 - mine, 3 - outer
    top_in, top_out = excess == mine, excess == outer
    top_far_in, top_far_out = excess == far_in, excess == far_out

    pair = lambda value: lax.ppermute(value, "job", PAIR)
    middle = lambda value: lax.ppermute(value, "job", MIDDLE)
    shift = lambda value, d: lax.ppermute(value, "job", [(i, (i + d) % JOBS) for i in range(JOBS)])
    across = lambda value: lax.ppermute(value, "tensor", TENSOR_X)
    beside = lambda value: lax.ppermute(value, "tensor", TENSOR_CORE)

    low, high = turn(adapter_down[0], tile)
    s1 = pair(low)
    m1 = middle(low)

    up = adapter_up[0]
    g0 = grad_out[0]
    up_z = jnp.stack([up] + [shift(up, d) for d in (1, 2, 3)])
    g2 = across(g0)
    g1 = beside(g0)
    up_x = across(up_z)
    g3 = beside(g2)
    up_c = beside(jnp.stack([up_z, up_x]))
    grads = (g0, g1, g2, g3)
    ups = (up_z, up_c[0], up_x, up_c[1])

    s2 = pair(jnp.where(inner & ~top_in, m1, high))
    m2 = middle(jnp.where(top_in, high, s1))

    parts, wide = pull(tables, place, grads, ups, features, norm, tile)

    def chunk(index):
        return lax.dynamic_slice_in_dim(parts, index * half, half, 0)

    def added(index, value, use):
        return (chunk(index).astype(F32) + jnp.where(use, value.astype(F32), 0.0)).astype(BF16)

    spare = CHUNKS - 1
    c4 = jnp.where(top_in | top_far_in, far_out, spare)
    c3 = jnp.where(top_in, far_in, jnp.where(top_far_in, spare, far_out))
    s3 = pair(jnp.where(inner, jnp.where(top_in, m1, m2), chunk(c4)))
    m3 = middle(jnp.where(top_in, s1, s2))
    s4 = pair(jnp.where(inner, jnp.where(top_in, m2, m3), chunk(c3)))
    n3 = middle(added(jnp.where(top_far_in, far_out, spare), s3, ~top_in))

    none = jnp.int32(CHUNKS + 1)
    here = [
        jnp.where(inner, mine, outer),
        jnp.where(excess == z, spare, none),
        jnp.where(inner, outer, mine),
        jnp.where(
            inner, jnp.where(top_out, spare, none), jnp.where(top_in, spare, far_in)
        ),
        jnp.where(inner, none, jnp.where(top_in, far_in, jnp.where(top_far_in, spare, far_out))),
        jnp.where(
            inner, none, jnp.where(top_in | top_far_in, far_out, jnp.where(top_far_out, spare, none))
        ),
        jnp.where(inner, far_in, none),
        jnp.where(inner, jnp.where(top_far_in, spare, far_out), none),
        jnp.where(
            inner, jnp.where(top_far_in, far_out, jnp.where(top_far_out, spare, none)), none
        ),
    ]
    where_to = jnp.stack(here).astype(jnp.int32)
    partial, table = project(
        block_adapter, owner_slot, where_to, (low, high, s1, s2, s3, s4, m1, m2, m3), features, 512
    )
    both = (partial.astype(F32) + beside(partial).astype(F32)).astype(BF16)
    other = across(both)

    grad_rows = base(block_length, place, grads, wide, value_weight, table, tile)

    s5 = pair(
        jnp.where(
            inner,
            added(spare, n3, ~top_in),
            chunk(jnp.where(top_in, spare, far_in)),
        )
    )
    n2 = middle(added(jnp.where(top_far_in, spare, far_out), jnp.where(top_in, s3, s4), True))
    s6 = pair(
        jnp.where(inner, added(outer, jnp.where(top_in, n3, n2), True), chunk(mine))
    )
    n1 = middle(added(far_in, jnp.where(top_in, s4, s5), True))

    ours = part_up(tables, place, grads, (both, other), norm)
    theirs = [shift(ours[d], d) for d in (1, 2, 3)]
    grad_up = ours[0].astype(F32)
    for value in theirs:
        grad_up = grad_up + value.astype(F32)

    grad_down = last(place, parts, s6, n1, s5, n2, tile)
    return (grad_rows[None], grad_down[None], grad_up[None])


def block_tables(block_ids, block_sizes, owner_slot, adapter_rank, block_rows, rank_width):
    adapter_count = owner_slot.shape[0]
    matches = (block_ids[:, None] == jnp.arange(adapter_count, dtype=jnp.int32)[None, :]).astype(
        jnp.int32
    )
    slot_index = jnp.sum(matches * owner_slot[None, :], axis=1)
    rank_used = jnp.sum(matches * adapter_rank[None, :], axis=1)
    selector = (slot_index[:, None] == jnp.arange(adapter_count, dtype=jnp.int32)[None, :]).astype(F32)
    live_rows = (jnp.arange(block_rows, dtype=jnp.int32)[None, :] < block_sizes[:, None]).astype(F32)
    keep_ranks = (jnp.arange(rank_width, dtype=jnp.int32)[None, :] < rank_used[:, None]).astype(F32)
    scaling = rank_width / (2.0 * rank_used.astype(F32))
    factor = live_rows[:, :, None] * keep_ranks[:, None, :] * scaling[:, None, None]
    return (slot_index, selector, live_rows, factor)


def on_any_device(
    inputs,
    grad_out,
    value_weight,
    adapter_down,
    adapter_up,
    block_adapter,
    block_length,
    owner_slot,
    adapter_rank,
):
    highest = lax.Precision.HIGHEST
    features = inputs[0]
    row_count, local_width = features.shape
    block_count = block_adapter.shape[1]
    block_rows = row_count // block_count
    rank_width = adapter_down.shape[2]
    local_values = adapter_up.shape[1]
    norm = 1.0 / math.sqrt(lax.axis_size("job") * row_count)
    cotangent = lax.all_gather(grad_out, "tensor", axis=1, tiled=True)[0]
    slot_index, selector, live_rows, factor = block_tables(
        block_adapter[0], block_length[0], owner_slot, adapter_rank, block_rows, rank_width
    )
    base_term = lax.dot_general(
        cotangent, value_weight, (((1,), (1,)), ((), ())), preferred_element_type=F32
    )
    value_start = lax.axis_index("tensor") * local_values
    cot_slice = lax.dynamic_slice_in_dim(cotangent, value_start, local_values, 1).reshape(
        block_count, block_rows, local_values
    )
    feat_blocks = features.reshape(block_count, block_rows, local_width)
    down_all = lax.all_gather(adapter_down, "job", axis=0, tiled=True)
    up_all = lax.all_gather(adapter_up, "job", axis=0, tiled=True)
    down_used = jnp.take(down_all, slot_index, axis=0)
    up_used = jnp.take(up_all, slot_index, axis=0)
    projected = jnp.einsum("btd,bdr->btr", feat_blocks, down_used, preferred_element_type=F32)
    pulled = jnp.einsum("btk,bkr->btr", cot_slice, up_used, preferred_element_type=F32)
    projected = lax.psum(projected.astype(BF16), "tensor").astype(F32)
    pulled = lax.psum(pulled.astype(BF16), "tensor").astype(F32)
    low_down = (projected * factor).astype(BF16)
    low_grad = (pulled * factor).astype(BF16)
    adapter_term = jnp.einsum(
        "btr,bdr->btd", low_grad, down_used, preferred_element_type=F32
    ).reshape(row_count, local_width)
    grad_rows = (base_term * live_rows.reshape(row_count)[:, None] + adapter_term).astype(BF16)[None]
    block_down = jnp.einsum("btd,btr->bdr", feat_blocks, low_grad, preferred_element_type=F32)
    block_up = jnp.einsum("btk,btr->bkr", cot_slice, low_down, preferred_element_type=F32)
    part_down = jnp.einsum("bs,bdr->sdr", selector, block_down, precision=highest) * norm
    part_up_sum = jnp.einsum("bs,bkr->skr", selector, block_up, precision=highest) * norm
    grad_down = lax.psum_scatter(part_down.astype(BF16), "job", scatter_dimension=0, tiled=True).astype(F32)
    grad_up = lax.psum_scatter(part_up_sum.astype(BF16), "job", scatter_dimension=0, tiled=True).astype(F32)
    return (grad_rows, grad_down, grad_up)


def solution(mesh):
    placed = (
        P(("groups", "job"), None, "tensor"),
        P(("groups", "job"), "tensor", None),
        P("tensor", None),
        P(("groups", "job"), "tensor", None),
        P(("groups", "job"), "tensor", None),
        P(("groups", "job"), None),
        P(("groups", "job"), None),
        P("groups"),
        P("groups"),
    )
    small = mesh.shape["job"] == JOBS and mesh.shape["tensor"] == 4
    return jax.shard_map(
        on_device if small else on_any_device,
        mesh=mesh,
        in_specs=placed,
        out_specs=(
            P(("groups", "job"), None, "tensor"),
            P(("groups", "job"), "tensor", None),
            P(("groups", "job"), "tensor", None),
        ),
        check_vma=False,
    )
```

```python
import functools
import math

import jax
import jax.numpy as jnp
from jax import lax
from jax.experimental import pallas as pl
from jax.experimental.pallas import tpu as pltpu
from jax.sharding import PartitionSpec as P

F32 = jnp.float32
BF16 = jnp.bfloat16
VMEM_LIMIT = 60 * 1024 * 1024
CHUNKS = 5
JOBS = 4
PAIR = [(0, 1), (1, 0), (2, 3), (3, 2)]
MIDDLE = [
    pair
    for t in range(4)
    for pair in ((t * 4 + 1, t * 4 + 2), (t * 4 + 2, t * 4 + 1), (t * 4, (t ^ 1) * 4), (t * 4 + 3, (t ^ 1) * 4 + 3))
]
TENSOR_X = [(0, 2), (2, 0), (1, 3), (3, 1)]
TENSOR_CORE = [(0, 1), (1, 0), (2, 3), (3, 2)]


def params():
    return pltpu.CompilerParams(vmem_limit_bytes=VMEM_LIMIT)


def cost(flops, moved):
    return pl.CostEstimate(flops=flops, bytes_accessed=moved, transcendentals=0)


def whole(shape):
    return pl.BlockSpec(shape, lambda *_: (0,) * len(shape))


def smem():
    return pl.BlockSpec(memory_space=pltpu.SMEM)


def turn_kernel(down_ref, low_ref, high_ref):
    turned = down_ref[...].T
    half = low_ref.shape[0]
    low_ref[...] = turned[:half]
    high_ref[...] = turned[half:]


def turn(down, tile):
    width, rank = down.shape
    half = rank // 2
    out = jax.ShapeDtypeStruct((half, width), down.dtype)
    return pl.pallas_call(
        turn_kernel,
        grid=(width // tile,),
        in_specs=[pl.BlockSpec((tile, rank), lambda i: (i, 0))],
        out_specs=[pl.BlockSpec((half, tile), lambda i: (0, i))] * 2,
        out_shape=[out, out],
        compiler_params=params(),
        cost_estimate=cost(0, 4 * width * rank),
        name="turn_adapter",
    )(down)


def block_factor(ids, lengths, owners, ranks, b, rows, width):
    adapter = ids[0, b]
    rank = ranks[adapter]
    live = lax.broadcasted_iota(jnp.int32, (rows, width), 0) < lengths[0, b]
    keep = lax.broadcasted_iota(jnp.int32, (rows, width), 1) < rank
    scale = jnp.float32(width) / (2.0 * rank.astype(F32))
    return owners[adapter], jnp.where(live & keep, scale, 0.0)


def spread(low, slot):
    half = low.shape[1] // 2
    lanes = lax.broadcasted_iota(jnp.int32, low.shape, 1)
    turned = pltpu.roll(low, half, 1)
    twice = jnp.where(lanes < half, low, turned)
    chunk = jnp.where(lanes < half, 0, 1)
    return jnp.concatenate(
        [
            jnp.where(chunk == slot, twice, 0.0),
            jnp.where(chunk + 2 == slot, twice, 0.0),
            jnp.where(lanes < half, turned, 0.0),
        ],
        axis=1,
    )


def gathered(full, slot, rank):
    half = rank // 2
    odd = lax.rem(slot, 2)
    both = jnp.where(slot >= 2, full[:, rank : 2 * rank], full[:, :rank])
    turned = pltpu.roll(both, half, 1)
    lower = jnp.where(odd == 1, turned, both)
    upper = pltpu.roll(full[:, 2 * rank :], half, 1)
    lanes = lax.broadcasted_iota(jnp.int32, both.shape, 1)
    return jnp.where(lanes < half, lower, upper)


def pull_kernel(norm, ids, lengths, owners, ranks, place, g0, g1, g2, g3, u0, u1, u2, u3, x_ref,
                part_ref, wide_ref, up, turned):
    t, z = place[0], place[1]
    quarter, values = g0.shape
    rank = u0.shape[2]
    block = x_ref.shape[0] // ids.shape[1]

    @pl.when(pl.program_id(0) == 0)
    def _():
        for q, u in enumerate((u0, u1, u2, u3)):
            start = pl.multiple_of(jnp.bitwise_xor(t, q) * quarter, quarter)
            for d in range(JOBS):
                slot = lax.rem(z - d + JOBS, JOBS)
                up[slot, pl.ds(start, quarter), :] = u[d]
        for q, g in enumerate((g0, g1, g2, g3)):
            for j in range(quarter // block):
                b = jnp.bitwise_xor(t, q) * (quarter // block) + j
                slot, factor = block_factor(ids, lengths, owners, ranks, b, block, rank)
                pulled = jnp.dot(g[j * block : (j + 1) * block, :], up[slot], preferred_element_type=F32)
                low = spread((pulled * factor).astype(BF16).astype(F32), slot)
                rows = pl.ds(pl.multiple_of(b * block, block), block)
                wide_ref[rows, :] = low.astype(BF16)
                turned[:, rows] = low.T.astype(BF16)

    used = part_ref.shape[0]
    part_ref[...] = (
        jnp.dot(turned[:used, :], x_ref[...], preferred_element_type=F32) * norm
    ).astype(BF16)


def pull(tables, place, grads, ups, features, norm, tile):
    rows, width = features.shape
    quarter, values = grads[0].shape
    rank = ups[0].shape[2]
    used = CHUNKS * rank // 2
    return pl.pallas_call(
        functools.partial(pull_kernel, norm),
        grid=(width // tile,),
        in_specs=[smem()] * 5
        + [whole((quarter, values))] * 4
        + [whole((JOBS, quarter, rank))] * 4
        + [pl.BlockSpec((rows, tile), lambda i: (0, i))],
        out_specs=[
            pl.BlockSpec((used, tile), lambda i: (0, i)),
            whole((rows, 3 * rank)),
        ],
        out_shape=[
            jax.ShapeDtypeStruct((used, width), BF16),
            jax.ShapeDtypeStruct((rows, 3 * rank), BF16),
        ],
        scratch_shapes=[
            pltpu.VMEM((JOBS, values, rank), BF16),
            pltpu.VMEM((3 * rank, rows), BF16),
        ],
        compiler_params=params(),
        cost_estimate=cost(2 * used * rows * width, 2 * (rows * width + used * width + 2 * rows * values)),
        name="pull_and_part_down",
    )(*tables, place, *grads, *ups, features)


def arrivals(z, excess):
    inner = (z == 1) | (z == 2)
    mine = jnp.where(z < 2, 1, 2)
    outer = jnp.where(z < 2, 0, 3)
    far_in, far_out = 3 - mine, 3 - outer
    top_in, top_out = excess == mine, excess == outer
    top_far_in, top_far_out = excess == far_in, excess == far_out
    spare, none = CHUNKS - 1, CHUNKS + 1
    return [
        z,
        jnp.where(excess == z, spare, none),
        jnp.where(inner, outer, mine),
        jnp.where(inner, jnp.where(top_out, spare, none), jnp.where(top_in, spare, far_in)),
        jnp.where(inner, none, jnp.where(top_in, far_in, jnp.where(top_far_in, spare, far_out))),
        jnp.where(
            inner, none, jnp.where(top_in | top_far_in, far_out, jnp.where(top_far_out, spare, none))
        ),
        jnp.where(inner, far_in, none),
        jnp.where(inner, jnp.where(top_far_in, spare, far_out), none),
        jnp.where(
            inner, jnp.where(top_far_in, far_out, jnp.where(top_far_out, spare, none)), none
        ),
    ]


def project_kernel(ids, owners, place, *refs):
    chunks = refs[:9]
    x_ref, out_ref, table_ref, sems = refs[9:]
    half, width = chunks[0].shape
    rank = 2 * half
    rows = x_ref.shape[0]
    block = rank

    @pl.when(pl.program_id(0) == 0)
    def _():
        where_to = arrivals(place[1], place[2])
        for k, chunk in enumerate(chunks):
            spot = where_to[k]

            @pl.when(spot < CHUNKS)
            def _():
                start = pl.multiple_of(spot * half, half)
                pltpu.make_async_copy(chunk, table_ref.at[pl.ds(start, half), :], sems.at[k]).start()

        table_ref[CHUNKS * half :, :] = jnp.zeros((half, width), BF16)
        for k, chunk in enumerate(chunks):
            spot = where_to[k]

            @pl.when(spot < CHUNKS)
            def _():
                start = pl.multiple_of(spot * half, half)
                pltpu.make_async_copy(chunk, table_ref.at[pl.ds(start, half), :], sems.at[k]).wait()

    full = lax.dot_general(
        x_ref[...], table_ref[...], (((1,), (1,)), ((), ())), preferred_element_type=F32
    )
    first = pl.program_id(0) * (rows // block)
    for j in range(rows // block):
        slot = owners[ids[0, first + j]]
        piece = gathered(full[j * block : (j + 1) * block], slot, rank)
        out_ref[j * block : (j + 1) * block, :] = piece.astype(BF16)


def project(ids, owners, place, chunks, features, tile):
    rows, width = features.shape
    half = chunks[0].shape[0]
    return pl.pallas_call(
        project_kernel,
        grid=(rows // tile,),
        in_specs=[smem()] * 3
        + [pl.BlockSpec(memory_space=pl.ANY)] * 9
        + [pl.BlockSpec((tile, width), lambda i: (i, 0))],
        out_specs=[
            pl.BlockSpec((tile, 2 * half), lambda i: (i, 0)),
            whole((6 * half, width)),
        ],
        out_shape=[
            jax.ShapeDtypeStruct((rows, 2 * half), BF16),
            jax.ShapeDtypeStruct((6 * half, width), BF16),
        ],
        scratch_shapes=[pltpu.SemaphoreType.DMA((9,))],
        compiler_params=params(),
        cost_estimate=cost(2 * 6 * half * rows * width, 2 * (rows * width + 12 * half * width)),
        name="project",
    )(ids, owners, place, *chunks, features)


def base_kernel(lengths, place, g0, g1, g2, g3, weight_ref, out_ref):
    t = place[0]
    quarter, values = g0.shape
    block = out_ref.shape[0] // lengths.shape[1]
    tile = out_ref.shape[1]
    for q, g in enumerate((g0, g1, g2, g3)):
        start = pl.multiple_of(jnp.bitwise_xor(t, q) * quarter, quarter)
        term = lax.dot_general(
            g[...], weight_ref[...], (((1,), (1,)), ((), ())), preferred_element_type=F32
        )
        for j in range(quarter // block):
            b = jnp.bitwise_xor(t, q) * (quarter // block) + j
            live = lax.broadcasted_iota(jnp.int32, (block, tile), 0) < lengths[0, b]
            out_ref[pl.ds(pl.multiple_of(start + j * block, block), block), :] = jnp.where(
                live, term[j * block : (j + 1) * block], 0.0
            ).astype(BF16)


def base(lengths, place, grads, weight, half_index, tile):
    width, values = weight.shape[0] // 2, weight.shape[1]
    quarter = grads[0].shape[0]
    rows = 4 * quarter
    first = half_index * (width // tile)
    return pl.pallas_call(
        base_kernel,
        grid=(width // tile,),
        in_specs=[smem()] * 2
        + [whole((quarter, values))] * 4
        + [pl.BlockSpec((tile, values), lambda i: (first + i, 0))],
        out_specs=pl.BlockSpec((rows, tile), lambda i: (0, i)),
        out_shape=jax.ShapeDtypeStruct((rows, width), BF16),
        compiler_params=params(),
        cost_estimate=cost(2 * rows * width * values, 2 * (rows * values + width * values + rows * width)),
        name="base_term",
    )(lengths, place, *grads, weight)


def rows_kernel(wide_ref, table_ref, first_ref, second_ref, out_ref):
    term = jnp.dot(wide_ref[...], table_ref[...], preferred_element_type=F32)
    late = pl.program_id(0) >= pl.num_programs(0) // 2

    @pl.when(jnp.logical_not(late))
    def _():
        out_ref[...] = (first_ref[...].astype(F32) + term).astype(BF16)

    @pl.when(late)
    def _():
        out_ref[...] = (second_ref[...].astype(F32) + term).astype(BF16)


def add_rows(wide, table, halves, tile):
    rows, deep = wide.shape
    width = table.shape[1]
    steps = width // tile
    half = steps // 2
    return pl.pallas_call(
        rows_kernel,
        grid=(steps,),
        in_specs=[
            whole((rows, deep)),
            pl.BlockSpec((deep, tile), lambda i: (0, i)),
            pl.BlockSpec((rows, tile), lambda i: (0, jnp.minimum(i, half - 1))),
            pl.BlockSpec((rows, tile), lambda i: (0, jnp.maximum(i - half, 0))),
        ],
        out_specs=pl.BlockSpec((rows, tile), lambda i: (0, i)),
        out_shape=jax.ShapeDtypeStruct((rows, width), BF16),
        compiler_params=params(),
        cost_estimate=cost(2 * rows * width * deep, 2 * (2 * rows * width + deep * (rows + width))),
        name="grad_rows",
    )(wide, table, *halves)


def part_up_kernel(norm, ids, lengths, owners, ranks, place, g0, g1, g2, g3, a_ref, b_ref, *rest):
    outs, (slice_ref, wide) = rest[:JOBS], rest[JOBS:]
    t, z, excess = place[0], place[1], place[2]
    quarter, values = g0.shape
    rank = a_ref.shape[1]
    half = rank // 2
    block = a_ref.shape[0] // ids.shape[1]
    columns = pl.ds(pl.multiple_of(t * quarter, quarter), quarter)
    for q, g in enumerate((g0, g1, g2, g3)):
        start = pl.multiple_of(jnp.bitwise_xor(t, q) * quarter, quarter)
        slice_ref[pl.ds(start, quarter), :] = g[:, columns]
    for b in range(ids.shape[1]):
        slot, factor = block_factor(ids, lengths, owners, ranks, b, block, rank)
        rows = slice(b * block, (b + 1) * block)
        low = (a_ref[rows, :].astype(F32) + b_ref[rows, :].astype(F32)) * factor
        wide[rows, :] = spread(low.astype(BF16).astype(F32), slot).astype(BF16)
    full = (
        lax.dot_general(slice_ref[...], wide[...], (((0,), (0,)), ((), ())), preferred_element_type=F32) * norm
    )
    lanes = lax.broadcasted_iota(jnp.int32, (quarter, rank), 1)
    for d, out in enumerate(outs):
        slot = lax.rem(z + d, JOBS)
        keep = jnp.where(slot == excess, rank, half)
        out[...] = jnp.where(lanes < keep, gathered(full, slot, rank), 0.0).astype(BF16)


def part_up(tables, place, grads, sums, norm):
    quarter, values = grads[0].shape
    rows, rank = sums[0].shape
    vmem = pl.BlockSpec(memory_space=pltpu.VMEM)
    return pl.pallas_call(
        functools.partial(part_up_kernel, norm),
        in_specs=[smem()] * 5 + [vmem] * 6,
        out_specs=[vmem] * JOBS,
        out_shape=[jax.ShapeDtypeStruct((quarter, rank), BF16)] * JOBS,
        scratch_shapes=[
            pltpu.VMEM((rows, quarter), BF16),
            pltpu.VMEM((rows, 3 * rank), BF16),
        ],
        compiler_params=params(),
        cost_estimate=cost(2 * rows * quarter * 3 * rank, 2 * (rows * values + 2 * rows * rank)),
        name="part_up",
    )(*tables, place, *grads, *sums)


def last_kernel(place, own0, own1, t1, n1, t2, n2, out_ref):
    half = own0.shape[0]
    rank = 2 * half
    total = (
        jnp.concatenate([own0[...], own1[...]], axis=0).astype(F32)
        + jnp.concatenate([t1[...], t2[...]], axis=0).astype(F32)
    )
    inner = (place[1] == 1) | (place[1] == 2)
    total += jnp.where(inner, jnp.concatenate([n1[...], n2[...]], axis=0).astype(F32), 0.0)
    keep = jnp.where(place[1] == place[2], rank, half)
    rows = lax.broadcasted_iota(jnp.int32, total.shape, 0)
    out_ref[...] = jnp.where(rows < keep, total, 0.0).T


def last(place, parts, t1, n1, t2, n2, tile):
    half, width = t1.shape
    piece = pl.BlockSpec((half, tile), lambda i, place: (0, i))
    return pl.pallas_call(
        last_kernel,
        grid_spec=pltpu.PrefetchScalarGridSpec(
            num_scalar_prefetch=1,
            grid=(width // tile,),
            in_specs=[
                pl.BlockSpec((half, tile), lambda i, place: (place[1], i)),
                pl.BlockSpec((half, tile), lambda i, place: (CHUNKS - 1, i)),
            ]
            + [piece] * 4,
            out_specs=pl.BlockSpec((tile, 2 * half), lambda i, place: (i, 0)),
        ),
        out_shape=jax.ShapeDtypeStruct((width, 2 * half), F32),
        compiler_params=params(),
        cost_estimate=cost(0, 2 * 6 * half * width + 8 * half * width),
        name="grad_down",
    )(place, parts, parts, t1, n1, t2, n2)


def on_device(
    inputs,
    grad_out,
    value_weight,
    adapter_down,
    adapter_up,
    block_adapter,
    block_length,
    owner_slot,
    adapter_rank,
):
    features = inputs[0]
    row_count, local_width = features.shape
    half = adapter_down.shape[2] // 2
    tile = 512
    norm = 1.0 / math.sqrt(JOBS * row_count)
    t, z = lax.axis_index("tensor"), lax.axis_index("job")
    excess = jnp.sum(jnp.where(adapter_rank > half, owner_slot, 0)).astype(jnp.int32)
    place = jnp.stack([t, z, excess]).astype(jnp.int32)
    tables = (block_adapter, block_length, owner_slot, adapter_rank)

    inner = (z == 1) | (z == 2)
    mine = jnp.where(z < 2, 1, 2)
    outer = jnp.where(z < 2, 0, 3)
    far_in, far_out = 3 - mine, 3 - outer
    top_in, top_out = excess == mine, excess == outer
    top_far_in, top_far_out = excess == far_in, excess == far_out

    pair = lambda value: lax.ppermute(value, "job", PAIR)
    middle = lambda value: lax.ppermute(value, ("tensor", "job"), MIDDLE)
    shift = lambda value, d: lax.ppermute(value, "job", [(i, (i + d) % JOBS) for i in range(JOBS)])
    across = lambda value: lax.ppermute(value, "tensor", TENSOR_X)
    beside = lambda value: lax.ppermute(value, "tensor", TENSOR_CORE)

    tie = lax.optimization_barrier

    up = adapter_up[0]
    g0 = grad_out[0]
    g2 = across(g0)
    g1 = beside(g0)
    up_z = jnp.stack([up] + [shift(up, d) for d in (1, 2, 3)])
    up_x = across(up_z)

    low, high = turn(adapter_down[0], local_width)
    s1 = pair(low)
    m1 = middle(low)

    s1, m1, up_x, g2, g1, up_z = tie((s1, m1, up_x, g2, g1, up_z))
    g3 = beside(g2)
    up_c = beside(jnp.stack([up_z, up_x]))
    s2 = pair(jnp.where(inner & ~top_in, m1, high))
    m2 = middle(jnp.where(top_in, high, s1))

    grads = (g0, g1, g2, g3)
    ups = (up_z, up_c[0], up_x, up_c[1])
    parts, wide = pull(tables, place, grads, ups, features, norm, 1024)

    def chunk(index):
        return lax.dynamic_slice_in_dim(parts, index * half, half, 0)

    def added(index, value, use):
        return (chunk(index).astype(F32) + jnp.where(use, value.astype(F32), 0.0)).astype(BF16)

    spare = CHUNKS - 1
    c4 = jnp.where(top_in | top_far_in, far_out, spare)
    c3 = jnp.where(top_in, far_in, jnp.where(top_far_in, spare, far_out))
    parts, s2, m2 = tie((parts, s2, m2))
    to_s3 = jnp.where(inner, jnp.where(top_in, m1, m2), chunk(c4))
    to_m3 = jnp.where(top_in, s1, s2)
    to_s3, to_m3, *grads = tie((to_s3, to_m3, *grads))
    s3 = pair(to_s3)
    m3 = middle(to_m3)
    base_a = base(block_length, place, grads, value_weight, 0, 768)
    s3, m3, base_a = tie((s3, m3, base_a))
    to_s4 = jnp.where(inner, jnp.where(top_in, m2, m3), chunk(c3))
    to_n3 = added(jnp.where(top_far_in, far_out, spare), s3, ~top_in)
    to_s4, to_n3, *grads = tie((to_s4, to_n3, *grads))
    s4 = pair(to_s4)
    n3 = middle(to_n3)
    base_b = base(block_length, place, grads, value_weight, 1, 768)
    s4, n3, base_b = tie((s4, n3, base_b))

    partial, table = project(
        block_adapter, owner_slot, place, (low, high, s1, s2, s3, s4, m1, m2, m3), features, 512
    )
    partial, s4, n3 = tie((partial, s4, n3))
    beyond = beside(partial)
    to_s5 = jnp.where(inner, added(spare, n3, ~top_in), chunk(jnp.where(top_in, spare, far_in)))
    to_n2 = added(jnp.where(top_far_in, spare, far_out), jnp.where(top_in, s3, s4), True)
    to_s5, to_n2, beyond = tie((to_s5, to_n2, beyond))
    s5 = pair(to_s5)
    n2 = middle(to_n2)
    both = (partial.astype(F32) + beyond.astype(F32)).astype(BF16)
    both, wide, table, base_a, base_b = tie((both, wide, table, base_a, base_b))
    other = across(both)
    grad_rows = add_rows(wide, table, (base_a, base_b), 512)
    grad_rows, s5, n2 = tie((grad_rows, s5, n2))

    to_s6 = jnp.where(inner, added(outer, jnp.where(top_in, n3, n2), True), chunk(mine))
    to_n1 = added(far_in, jnp.where(top_in, s4, s5), True)
    to_s6, to_n1, other = tie((to_s6, to_n1, other))
    s6 = pair(to_s6)
    n1 = middle(to_n1)

    ours = part_up(tables, place, grads, (both, other), norm)
    theirs = [shift(ours[d], d) for d in (1, 2, 3)]
    grad_up = ours[0].astype(F32)
    for value in theirs:
        grad_up = grad_up + value.astype(F32)

    grad_down = last(place, parts, s6, n1, s5, n2, 1024)
    return (grad_rows[None], grad_down[None], grad_up[None])


def block_tables(block_ids, block_sizes, owner_slot, adapter_rank, block_rows, rank_width):
    adapter_count = owner_slot.shape[0]
    matches = (block_ids[:, None] == jnp.arange(adapter_count, dtype=jnp.int32)[None, :]).astype(
        jnp.int32
    )
    slot_index = jnp.sum(matches * owner_slot[None, :], axis=1)
    rank_used = jnp.sum(matches * adapter_rank[None, :], axis=1)
    selector = (slot_index[:, None] == jnp.arange(adapter_count, dtype=jnp.int32)[None, :]).astype(F32)
    live_rows = (jnp.arange(block_rows, dtype=jnp.int32)[None, :] < block_sizes[:, None]).astype(F32)
    keep_ranks = (jnp.arange(rank_width, dtype=jnp.int32)[None, :] < rank_used[:, None]).astype(F32)
    scaling = rank_width / (2.0 * rank_used.astype(F32))
    factor = live_rows[:, :, None] * keep_ranks[:, None, :] * scaling[:, None, None]
    return (slot_index, selector, live_rows, factor)


def on_any_device(
    inputs,
    grad_out,
    value_weight,
    adapter_down,
    adapter_up,
    block_adapter,
    block_length,
    owner_slot,
    adapter_rank,
):
    highest = lax.Precision.HIGHEST
    features = inputs[0]
    row_count, local_width = features.shape
    block_count = block_adapter.shape[1]
    block_rows = row_count // block_count
    rank_width = adapter_down.shape[2]
    local_values = adapter_up.shape[1]
    norm = 1.0 / math.sqrt(lax.axis_size("job") * row_count)
    cotangent = lax.all_gather(grad_out, "tensor", axis=1, tiled=True)[0]
    slot_index, selector, live_rows, factor = block_tables(
        block_adapter[0], block_length[0], owner_slot, adapter_rank, block_rows, rank_width
    )
    base_term = lax.dot_general(
        cotangent, value_weight, (((1,), (1,)), ((), ())), preferred_element_type=F32
    )
    value_start = lax.axis_index("tensor") * local_values
    cot_slice = lax.dynamic_slice_in_dim(cotangent, value_start, local_values, 1).reshape(
        block_count, block_rows, local_values
    )
    feat_blocks = features.reshape(block_count, block_rows, local_width)
    down_all = lax.all_gather(adapter_down, "job", axis=0, tiled=True)
    up_all = lax.all_gather(adapter_up, "job", axis=0, tiled=True)
    down_used = jnp.take(down_all, slot_index, axis=0)
    up_used = jnp.take(up_all, slot_index, axis=0)
    projected = jnp.einsum("btd,bdr->btr", feat_blocks, down_used, preferred_element_type=F32)
    pulled = jnp.einsum("btk,bkr->btr", cot_slice, up_used, preferred_element_type=F32)
    projected = lax.psum(projected.astype(BF16), "tensor").astype(F32)
    pulled = lax.psum(pulled.astype(BF16), "tensor").astype(F32)
    low_down = (projected * factor).astype(BF16)
    low_grad = (pulled * factor).astype(BF16)
    adapter_term = jnp.einsum(
        "btr,bdr->btd", low_grad, down_used, preferred_element_type=F32
    ).reshape(row_count, local_width)
    grad_rows = (base_term * live_rows.reshape(row_count)[:, None] + adapter_term).astype(BF16)[None]
    block_down = jnp.einsum("btd,btr->bdr", feat_blocks, low_grad, preferred_element_type=F32)
    block_up = jnp.einsum("btk,btr->bkr", cot_slice, low_down, preferred_element_type=F32)
    part_down = jnp.einsum("bs,bdr->sdr", selector, block_down, precision=highest) * norm
    part_up_sum = jnp.einsum("bs,bkr->skr", selector, block_up, precision=highest) * norm
    grad_down = lax.psum_scatter(part_down.astype(BF16), "job", scatter_dimension=0, tiled=True).astype(F32)
    grad_up = lax.psum_scatter(part_up_sum.astype(BF16), "job", scatter_dimension=0, tiled=True).astype(F32)
    return (grad_rows, grad_down, grad_up)


def solution(mesh):
    placed = (
        P(("groups", "job"), None, "tensor"),
        P(("groups", "job"), "tensor", None),
        P("tensor", None),
        P(("groups", "job"), "tensor", None),
        P(("groups", "job"), "tensor", None),
        P(("groups", "job"), None),
        P(("groups", "job"), None),
        P("groups"),
        P("groups"),
    )
    small = mesh.shape["job"] == JOBS and mesh.shape["tensor"] == 4
    return jax.shard_map(
        on_device if small else on_any_device,
        mesh=mesh,
        in_specs=placed,
        out_specs=(
            P(("groups", "job"), None, "tensor"),
            P(("groups", "job"), "tensor", None),
            P(("groups", "job"), "tensor", None),
        ),
        check_vma=False,
    )
```

```python
import functools
import math

import jax
import jax.numpy as jnp
from jax import lax
from jax.experimental import pallas as pl
from jax.experimental.pallas import tpu as pltpu
from jax.sharding import PartitionSpec as P

F32 = jnp.float32
BF16 = jnp.bfloat16
VMEM_LIMIT = 28 * 1024 * 1024
CHUNKS = 5
JOBS = 4
PAIR = [(0, 1), (1, 0), (2, 3), (3, 2)]
MIDDLE = [
    pair
    for t in range(4)
    for pair in ((t * 4 + 1, t * 4 + 2), (t * 4 + 2, t * 4 + 1), (t * 4, (t ^ 1) * 4), (t * 4 + 3, (t ^ 1) * 4 + 3))
]
TENSOR_X = [(0, 2), (2, 0), (1, 3), (3, 1)]
TENSOR_CORE = [(0, 1), (1, 0), (2, 3), (3, 2)]


def params():
    return pltpu.CompilerParams(vmem_limit_bytes=VMEM_LIMIT)


def cost(flops, moved):
    return pl.CostEstimate(flops=flops, bytes_accessed=moved, transcendentals=0)


def whole(shape):
    return pl.BlockSpec(shape, lambda *_: (0,) * len(shape))


def far(value):
    return pltpu.with_memory_space_constraint(value, pltpu.HBM)


def smem():
    return pl.BlockSpec(memory_space=pltpu.SMEM)


def turn_kernel(down_ref, low_ref, high_ref):
    turned = down_ref[...].T
    half = low_ref.shape[0]
    low_ref[...] = turned[:half]
    high_ref[...] = turned[half:]


def turn(down, tile):
    width, rank = down.shape
    half = rank // 2
    out = jax.ShapeDtypeStruct((half, width), down.dtype)
    return pl.pallas_call(
        turn_kernel,
        grid=(width // tile,),
        in_specs=[pl.BlockSpec((tile, rank), lambda i: (i, 0))],
        out_specs=[pl.BlockSpec((half, tile), lambda i: (0, i))] * 2,
        out_shape=[out, out],
        compiler_params=params(),
        cost_estimate=cost(0, 4 * width * rank),
        name="turn_adapter",
    )(down)


def block_factor(ids, lengths, owners, ranks, b, rows, width):
    adapter = ids[0, b]
    rank = ranks[adapter]
    live = lax.broadcasted_iota(jnp.int32, (rows, width), 0) < lengths[0, b]
    keep = lax.broadcasted_iota(jnp.int32, (rows, width), 1) < rank
    scale = jnp.float32(width) / (2.0 * rank.astype(F32))
    return owners[adapter], jnp.where(live & keep, scale, 0.0)


def spread(low, slot):
    half = low.shape[1] // 2
    lanes = lax.broadcasted_iota(jnp.int32, low.shape, 1)
    turned = pltpu.roll(low, half, 1)
    twice = jnp.where(lanes < half, low, turned)
    chunk = jnp.where(lanes < half, 0, 1)
    return jnp.concatenate(
        [
            jnp.where(chunk == slot, twice, 0.0),
            jnp.where(chunk + 2 == slot, twice, 0.0),
            jnp.where(lanes < half, turned, 0.0),
        ],
        axis=1,
    )


def gathered(full, slot, rank):
    half = rank // 2
    odd = lax.rem(slot, 2)
    both = jnp.where(slot >= 2, full[:, rank : 2 * rank], full[:, :rank])
    turned = pltpu.roll(both, half, 1)
    lower = jnp.where(odd == 1, turned, both)
    upper = pltpu.roll(full[:, 2 * rank :], half, 1)
    lanes = lax.broadcasted_iota(jnp.int32, both.shape, 1)
    return jnp.where(lanes < half, lower, upper)


def roles(z, excess):
    inner = (z == 1) | (z == 2)
    mine = jnp.where(z < 2, 1, 2)
    far_in = 3 - mine
    far_out = jnp.where(z < 2, 3, 0)
    top_in, top_far_in = excess == mine, excess == far_in
    spare = CHUNKS - 1
    return [
        jnp.where(
            inner, jnp.where(top_far_in, far_out, spare), jnp.where(top_in | top_far_in, far_out, spare)
        ),
        jnp.where(
            inner,
            jnp.where(top_far_in, spare, far_out),
            jnp.where(top_in, far_in, jnp.where(top_far_in, spare, far_out)),
        ),
        jnp.where(inner | top_in, spare, far_in),
        jnp.bitwise_xor(z, 1),
        far_in,
        z,
        jnp.int32(spare),
    ]


def pull_kernel(norm, ids, lengths, owners, ranks, place, g0, g1, g2, g3, u0, u1, u2, u3, x_ref, *rest):
    parts, (wide_ref, up, turned, sums) = rest[:7], rest[7:]
    t, z = place[0], place[1]
    quarter, values = g0.shape
    rank = u0.shape[2]
    half = rank // 2
    block = x_ref.shape[0] // ids.shape[1]

    @pl.when(pl.program_id(0) == 0)
    def _():
        for q, u in enumerate((u0, u1, u2, u3)):
            start = pl.multiple_of(jnp.bitwise_xor(t, q) * quarter, quarter)
            for d in range(JOBS):
                slot = jnp.bitwise_xor(z, d)
                up[slot, pl.ds(start, quarter), :] = u[d]
        for q, g in enumerate((g0, g1, g2, g3)):
            for j in range(quarter // block):
                b = jnp.bitwise_xor(t, q) * (quarter // block) + j
                slot, factor = block_factor(ids, lengths, owners, ranks, b, block, rank)
                pulled = jnp.dot(g[j * block : (j + 1) * block, :], up[slot], preferred_element_type=F32)
                low = spread((pulled * factor).astype(BF16).astype(F32), slot)
                rows = pl.ds(pl.multiple_of(b * block, block), block)
                wide_ref[rows, :] = low.astype(BF16)
                turned[:, rows] = low.T.astype(BF16)

    sums[...] = (
        jnp.dot(turned[: CHUNKS * half, :], x_ref[...], preferred_element_type=F32) * norm
    ).astype(BF16)
    for part, chunk in zip(parts, roles(z, place[2])):
        part[...] = sums[pl.ds(pl.multiple_of(chunk * half, half), half), :]


def pull(tables, place, grads, ups, features, norm, tile):
    rows, width = features.shape
    quarter, values = grads[0].shape
    rank = ups[0].shape[2]
    used = CHUNKS * rank // 2
    return pl.pallas_call(
        functools.partial(pull_kernel, norm),
        grid=(width // tile,),
        in_specs=[smem()] * 5
        + [whole((quarter, values))] * 4
        + [whole((JOBS, quarter, rank))] * 4
        + [pl.BlockSpec((rows, tile), lambda i: (0, i))],
        out_specs=[pl.BlockSpec((rank // 2, tile), lambda i: (0, i))] * 7 + [whole((rows, 3 * rank))],
        out_shape=[jax.ShapeDtypeStruct((rank // 2, width), BF16)] * 7
        + [jax.ShapeDtypeStruct((rows, 3 * rank), BF16)],
        scratch_shapes=[
            pltpu.VMEM((JOBS, values, rank), BF16),
            pltpu.VMEM((3 * rank, rows), BF16),
            pltpu.VMEM((used, tile), BF16),
        ],
        compiler_params=params(),
        cost_estimate=cost(2 * used * rows * width, 2 * (rows * width + used * width + 2 * rows * values)),
        name="pull_and_part_down",
    )(*tables, place, *map(far, grads), *ups, far(features))


def arrivals(z, excess):
    inner = (z == 1) | (z == 2)
    mine = jnp.where(z < 2, 1, 2)
    outer = jnp.where(z < 2, 0, 3)
    far_in, far_out = 3 - mine, 3 - outer
    top_in, top_out = excess == mine, excess == outer
    top_far_in, top_far_out = excess == far_in, excess == far_out
    spare, none = CHUNKS - 1, CHUNKS + 1
    return [
        z,
        jnp.where(excess == z, spare, none),
        jnp.where(inner, outer, mine),
        jnp.where(inner, jnp.where(top_out, spare, none), jnp.where(top_in, spare, far_in)),
        jnp.where(inner, none, jnp.where(top_in, far_in, jnp.where(top_far_in, spare, far_out))),
        jnp.where(
            inner, none, jnp.where(top_in | top_far_in, far_out, jnp.where(top_far_out, spare, none))
        ),
        jnp.where(inner, far_in, none),
        jnp.where(inner, jnp.where(top_far_in, spare, far_out), none),
        jnp.where(
            inner, jnp.where(top_far_in, far_out, jnp.where(top_far_out, spare, none)), none
        ),
    ]


def project_kernel(ids, owners, place, *refs):
    chunks = refs[:9]
    x_ref, out_ref, table_ref, sems = refs[9:]
    half, width = chunks[0].shape
    rank = 2 * half
    rows = x_ref.shape[0]
    block = rank

    @pl.when(pl.program_id(0) == 0)
    def _():
        where_to = arrivals(place[1], place[2])
        for k, chunk in enumerate(chunks):
            spot = where_to[k]

            @pl.when(spot < CHUNKS)
            def _():
                start = pl.multiple_of(spot * half, half)
                pltpu.make_async_copy(chunk, table_ref.at[pl.ds(start, half), :], sems.at[k]).start()

        table_ref[CHUNKS * half :, :] = jnp.zeros((half, width), BF16)
        for k, chunk in enumerate(chunks):
            spot = where_to[k]

            @pl.when(spot < CHUNKS)
            def _():
                start = pl.multiple_of(spot * half, half)
                pltpu.make_async_copy(chunk, table_ref.at[pl.ds(start, half), :], sems.at[k]).wait()

    full = lax.dot_general(
        x_ref[...], table_ref[...], (((1,), (1,)), ((), ())), preferred_element_type=F32
    )
    first = pl.program_id(0) * (rows // block)
    for j in range(rows // block):
        slot = owners[ids[0, first + j]]
        piece = gathered(full[j * block : (j + 1) * block], slot, rank)
        out_ref[j * block : (j + 1) * block, :] = piece.astype(BF16)


def project(ids, owners, place, chunks, features, tile):
    rows, width = features.shape
    half = chunks[0].shape[0]
    return pl.pallas_call(
        project_kernel,
        grid=(rows // tile,),
        in_specs=[smem()] * 3
        + [pl.BlockSpec(memory_space=pl.ANY)] * 9
        + [pl.BlockSpec((tile, width), lambda i: (i, 0))],
        out_specs=[
            pl.BlockSpec((tile, 2 * half), lambda i: (i, 0)),
            whole((6 * half, width)),
        ],
        out_shape=[
            jax.ShapeDtypeStruct((rows, 2 * half), BF16),
            jax.ShapeDtypeStruct((6 * half, width), BF16),
        ],
        scratch_shapes=[pltpu.SemaphoreType.DMA((9,))],
        compiler_params=params(),
        cost_estimate=cost(2 * 6 * half * rows * width, 2 * (rows * width + 12 * half * width)),
        name="project",
    )(ids, owners, place, *chunks, far(features))


def base_kernel(lengths, place, g0, g1, g2, g3, weight_ref, out_ref):
    t = place[0]
    quarter, values = g0.shape
    block = out_ref.shape[0] // lengths.shape[1]
    tile = out_ref.shape[1]
    for q, g in enumerate((g0, g1, g2, g3)):
        start = pl.multiple_of(jnp.bitwise_xor(t, q) * quarter, quarter)
        term = lax.dot_general(
            g[...], weight_ref[...], (((1,), (1,)), ((), ())), preferred_element_type=F32
        )
        for j in range(quarter // block):
            b = jnp.bitwise_xor(t, q) * (quarter // block) + j
            live = lax.broadcasted_iota(jnp.int32, (block, tile), 0) < lengths[0, b]
            out_ref[pl.ds(pl.multiple_of(start + j * block, block), block), :] = jnp.where(
                live, term[j * block : (j + 1) * block], 0.0
            ).astype(BF16)


def base(lengths, place, grads, weight, half_index, tile):
    width, values = weight.shape[0] // 2, weight.shape[1]
    quarter = grads[0].shape[0]
    rows = 4 * quarter
    first = half_index * (width // tile)
    return pl.pallas_call(
        base_kernel,
        grid=(width // tile,),
        in_specs=[smem()] * 2
        + [whole((quarter, values))] * 4
        + [pl.BlockSpec((tile, values), lambda i: (first + i, 0))],
        out_specs=pl.BlockSpec((rows, tile), lambda i: (0, i)),
        out_shape=jax.ShapeDtypeStruct((rows, width), BF16),
        compiler_params=params(),
        cost_estimate=cost(2 * rows * width * values, 2 * (rows * values + width * values + rows * width)),
        name="base_term",
    )(lengths, place, *map(far, grads), far(weight))


def rows_kernel(wide_ref, table_ref, first_ref, second_ref, out_ref):
    term = jnp.dot(wide_ref[...], table_ref[...], preferred_element_type=F32)
    late = pl.program_id(0) >= pl.num_programs(0) // 2

    @pl.when(jnp.logical_not(late))
    def _():
        out_ref[...] = (first_ref[...].astype(F32) + term).astype(BF16)

    @pl.when(late)
    def _():
        out_ref[...] = (second_ref[...].astype(F32) + term).astype(BF16)


def add_rows(wide, table, halves, tile):
    rows, deep = wide.shape
    width = table.shape[1]
    steps = width // tile
    half = steps // 2
    return pl.pallas_call(
        rows_kernel,
        grid=(steps,),
        in_specs=[
            whole((rows, deep)),
            pl.BlockSpec((deep, tile), lambda i: (0, i)),
            pl.BlockSpec((rows, tile), lambda i: (0, jnp.minimum(i, half - 1))),
            pl.BlockSpec((rows, tile), lambda i: (0, jnp.maximum(i - half, 0))),
        ],
        out_specs=pl.BlockSpec((rows, tile), lambda i: (0, i)),
        out_shape=jax.ShapeDtypeStruct((rows, width), BF16),
        compiler_params=params(),
        cost_estimate=cost(2 * rows * width * deep, 2 * (2 * rows * width + deep * (rows + width))),
        name="grad_rows",
    )(wide, table, *halves)


def part_up_kernel(norm, ids, lengths, owners, ranks, place, g0, g1, g2, g3, a_ref, b_ref, *rest):
    outs, (slice_ref, wide) = rest[:JOBS], rest[JOBS:]
    t, z, excess = place[0], place[1], place[2]
    quarter, values = g0.shape
    rank = a_ref.shape[1]
    half = rank // 2
    block = a_ref.shape[0] // ids.shape[1]
    columns = pl.ds(pl.multiple_of(t * quarter, quarter), quarter)
    for q, g in enumerate((g0, g1, g2, g3)):
        start = pl.multiple_of(jnp.bitwise_xor(t, q) * quarter, quarter)
        slice_ref[pl.ds(start, quarter), :] = g[:, columns]
    for b in range(ids.shape[1]):
        slot, factor = block_factor(ids, lengths, owners, ranks, b, block, rank)
        rows = slice(b * block, (b + 1) * block)
        low = (a_ref[rows, :].astype(F32) + b_ref[rows, :].astype(F32)) * factor
        wide[rows, :] = spread(low.astype(BF16).astype(F32), slot).astype(BF16)
    full = (
        lax.dot_general(slice_ref[...], wide[...], (((0,), (0,)), ((), ())), preferred_element_type=F32) * norm
    )
    lanes = lax.broadcasted_iota(jnp.int32, (quarter, rank), 1)
    for d, out in enumerate(outs):
        slot = jnp.bitwise_xor(z, d)
        keep = jnp.where(slot == excess, rank, half)
        out[...] = jnp.where(lanes < keep, gathered(full, slot, rank), 0.0).astype(BF16)


def part_up(tables, place, grads, sums, norm):
    quarter, values = grads[0].shape
    rows, rank = sums[0].shape
    vmem = pl.BlockSpec(memory_space=pltpu.VMEM)
    return pl.pallas_call(
        functools.partial(part_up_kernel, norm),
        in_specs=[smem()] * 5 + [vmem] * 6,
        out_specs=[vmem] * JOBS,
        out_shape=[jax.ShapeDtypeStruct((quarter, rank), BF16)] * JOBS,
        scratch_shapes=[
            pltpu.VMEM((rows, quarter), BF16),
            pltpu.VMEM((rows, 3 * rank), BF16),
        ],
        compiler_params=params(),
        cost_estimate=cost(2 * rows * quarter * 3 * rank, 2 * (rows * values + 2 * rows * rank)),
        name="part_up",
    )(*tables, place, *grads, *sums)


def last_kernel(place, own0, own1, t1, n1, t2, n2, out_ref):
    half = own0.shape[0]
    rank = 2 * half
    total = (
        jnp.concatenate([own0[...], own1[...]], axis=0).astype(F32)
        + jnp.concatenate([t1[...], t2[...]], axis=0).astype(F32)
    )
    inner = (place[1] == 1) | (place[1] == 2)
    total += jnp.where(inner, jnp.concatenate([n1[...], n2[...]], axis=0).astype(F32), 0.0)
    keep = jnp.where(place[1] == place[2], rank, half)
    rows = lax.broadcasted_iota(jnp.int32, total.shape, 0)
    out_ref[...] = jnp.where(rows < keep, total, 0.0).T


def last(place, own0, own1, t1, n1, t2, n2, tile):
    half, width = t1.shape
    piece = pl.BlockSpec((half, tile), lambda i, place: (0, i))
    return pl.pallas_call(
        last_kernel,
        grid_spec=pltpu.PrefetchScalarGridSpec(
            num_scalar_prefetch=1,
            grid=(width // tile,),
            in_specs=[piece] * 6,
            out_specs=pl.BlockSpec((tile, 2 * half), lambda i, place: (i, 0)),
        ),
        out_shape=jax.ShapeDtypeStruct((width, 2 * half), F32),
        compiler_params=params(),
        cost_estimate=cost(0, 2 * 6 * half * width + 8 * half * width),
        name="grad_down",
    )(place, own0, own1, t1, n1, t2, n2)


def on_device(
    inputs,
    grad_out,
    value_weight,
    adapter_down,
    adapter_up,
    block_adapter,
    block_length,
    owner_slot,
    adapter_rank,
):
    features = inputs[0]
    row_count, local_width = features.shape
    half = adapter_down.shape[2] // 2
    tile = 512
    norm = 1.0 / math.sqrt(JOBS * row_count)
    t, z = lax.axis_index("tensor"), lax.axis_index("job")
    excess = jnp.sum(jnp.where(adapter_rank > half, owner_slot, 0)).astype(jnp.int32)
    place = jnp.stack([t, z, excess]).astype(jnp.int32)
    tables = (block_adapter, block_length, owner_slot, adapter_rank)

    inner = (z == 1) | (z == 2)
    mine = jnp.where(z < 2, 1, 2)
    top_in = excess == mine

    pair = lambda value: lax.ppermute(value, "job", PAIR)
    middle = lambda value: lax.ppermute(value, ("tensor", "job"), MIDDLE)
    swap = lambda value, d: lax.ppermute(value, "job", [(i, i ^ d) for i in range(JOBS)])
    across = lambda value: lax.ppermute(value, "tensor", TENSOR_X)
    beside = lambda value: lax.ppermute(value, "tensor", TENSOR_CORE)

    tie = lax.optimization_barrier

    up = adapter_up[0]
    g0 = grad_out[0]
    g2 = across(g0)
    g1 = beside(g0)
    up_z = jnp.stack([up] + [swap(up, d) for d in (1, 2, 3)])
    up_x = across(up_z)

    low, high = turn(adapter_down[0], local_width)
    s1 = pair(low)
    m1 = middle(low)

    s1, m1, up_x, g2, g1, up_z = tie((s1, m1, up_x, g2, g1, up_z))
    g3 = beside(g2)
    up_c = beside(jnp.stack([up_z, up_x]))
    s2 = pair(jnp.where(inner & ~top_in, m1, high))
    m2 = middle(jnp.where(top_in, high, s1))

    grads = (g0, g1, g2, g3)
    ups = (up_z, up_c[0], up_x, up_c[1])
    *parts, wide = pull(tables, place, grads, ups, features, norm, 1024)

    def added(part, value, use=None):
        value = value.astype(F32)
        return (part.astype(F32) + (value if use is None else jnp.where(use, value, 0.0))).astype(BF16)

    *parts, s2, m2 = tie((*parts, s2, m2))
    to_s3 = jnp.where(inner, jnp.where(top_in, m1, m2), parts[0])
    to_m3 = jnp.where(top_in, s1, s2)
    to_s3, to_m3, *grads = tie((to_s3, to_m3, *grads))
    s3 = pair(to_s3)
    m3 = middle(to_m3)
    base_a = base(block_length, place, grads, value_weight, 0, 768)
    s3, m3, base_a = tie((s3, m3, base_a))
    to_s4 = jnp.where(inner, jnp.where(top_in, m2, m3), parts[1])
    to_n3 = added(parts[0], s3, ~top_in)
    to_s4, to_n3, *grads = tie((to_s4, to_n3, *grads))
    s4 = pair(to_s4)
    n3 = middle(to_n3)
    base_b = base(block_length, place, grads, value_weight, 1, 768)
    s4, n3, base_b = tie((s4, n3, base_b))

    partial, table = project(
        block_adapter, owner_slot, place, (low, high, s1, s2, s3, s4, m1, m2, m3), features, 512
    )
    partial, s4, n3 = tie((partial, s4, n3))
    beyond = beside(partial)
    to_s5 = added(parts[2], n3, inner & ~top_in)
    to_n2 = added(parts[1], jnp.where(top_in, s3, s4))
    to_s5, to_n2, beyond = tie((to_s5, to_n2, beyond))
    s5 = pair(to_s5)
    n2 = middle(to_n2)
    both = (partial.astype(F32) + beyond.astype(F32)).astype(BF16)
    both, wide, table, base_a, base_b = tie((both, wide, table, base_a, base_b))
    other = across(both)
    grad_rows = add_rows(wide, table, (base_a, base_b), 512)
    grad_rows, s5, n2 = tie((grad_rows, s5, n2))

    to_s6 = added(parts[3], jnp.where(top_in, n3, n2), inner)
    to_n1 = added(parts[4], jnp.where(top_in, s4, s5))
    to_s6, to_n1, other = tie((to_s6, to_n1, other))
    s6 = pair(to_s6)
    n1 = middle(to_n1)

    ours = part_up(tables, place, grads, (both, other), norm)
    theirs = [swap(ours[d], d) for d in (1, 2, 3)]
    grad_down = last(place, parts[5], parts[6], s6, n1, s5, n2, 1024)
    grad_down, *theirs = tie((grad_down, *theirs))
    grad_up = ours[0].astype(F32)
    for value in theirs:
        grad_up = grad_up + value.astype(F32)
    return (grad_rows[None], grad_down[None], grad_up[None])


def block_tables(block_ids, block_sizes, owner_slot, adapter_rank, block_rows, rank_width):
    adapter_count = owner_slot.shape[0]
    matches = (block_ids[:, None] == jnp.arange(adapter_count, dtype=jnp.int32)[None, :]).astype(
        jnp.int32
    )
    slot_index = jnp.sum(matches * owner_slot[None, :], axis=1)
    rank_used = jnp.sum(matches * adapter_rank[None, :], axis=1)
    selector = (slot_index[:, None] == jnp.arange(adapter_count, dtype=jnp.int32)[None, :]).astype(F32)
    live_rows = (jnp.arange(block_rows, dtype=jnp.int32)[None, :] < block_sizes[:, None]).astype(F32)
    keep_ranks = (jnp.arange(rank_width, dtype=jnp.int32)[None, :] < rank_used[:, None]).astype(F32)
    scaling = rank_width / (2.0 * rank_used.astype(F32))
    factor = live_rows[:, :, None] * keep_ranks[:, None, :] * scaling[:, None, None]
    return (slot_index, selector, live_rows, factor)


def on_any_device(
    inputs,
    grad_out,
    value_weight,
    adapter_down,
    adapter_up,
    block_adapter,
    block_length,
    owner_slot,
    adapter_rank,
):
    highest = lax.Precision.HIGHEST
    features = inputs[0]
    row_count, local_width = features.shape
    block_count = block_adapter.shape[1]
    block_rows = row_count // block_count
    rank_width = adapter_down.shape[2]
    local_values = adapter_up.shape[1]
    norm = 1.0 / math.sqrt(lax.axis_size("job") * row_count)
    cotangent = lax.all_gather(grad_out, "tensor", axis=1, tiled=True)[0]
    slot_index, selector, live_rows, factor = block_tables(
        block_adapter[0], block_length[0], owner_slot, adapter_rank, block_rows, rank_width
    )
    base_term = lax.dot_general(
        cotangent, value_weight, (((1,), (1,)), ((), ())), preferred_element_type=F32
    )
    value_start = lax.axis_index("tensor") * local_values
    cot_slice = lax.dynamic_slice_in_dim(cotangent, value_start, local_values, 1).reshape(
        block_count, block_rows, local_values
    )
    feat_blocks = features.reshape(block_count, block_rows, local_width)
    down_all = lax.all_gather(adapter_down, "job", axis=0, tiled=True)
    up_all = lax.all_gather(adapter_up, "job", axis=0, tiled=True)
    down_used = jnp.take(down_all, slot_index, axis=0)
    up_used = jnp.take(up_all, slot_index, axis=0)
    projected = jnp.einsum("btd,bdr->btr", feat_blocks, down_used, preferred_element_type=F32)
    pulled = jnp.einsum("btk,bkr->btr", cot_slice, up_used, preferred_element_type=F32)
    projected = lax.psum(projected.astype(BF16), "tensor").astype(F32)
    pulled = lax.psum(pulled.astype(BF16), "tensor").astype(F32)
    low_down = (projected * factor).astype(BF16)
    low_grad = (pulled * factor).astype(BF16)
    adapter_term = jnp.einsum(
        "btr,bdr->btd", low_grad, down_used, preferred_element_type=F32
    ).reshape(row_count, local_width)
    grad_rows = (base_term * live_rows.reshape(row_count)[:, None] + adapter_term).astype(BF16)[None]
    block_down = jnp.einsum("btd,btr->bdr", feat_blocks, low_grad, preferred_element_type=F32)
    block_up = jnp.einsum("btk,btr->bkr", cot_slice, low_down, preferred_element_type=F32)
    part_down = jnp.einsum("bs,bdr->sdr", selector, block_down, precision=highest) * norm
    part_up_sum = jnp.einsum("bs,bkr->skr", selector, block_up, precision=highest) * norm
    grad_down = lax.psum_scatter(part_down.astype(BF16), "job", scatter_dimension=0, tiled=True).astype(F32)
    grad_up = lax.psum_scatter(part_up_sum.astype(BF16), "job", scatter_dimension=0, tiled=True).astype(F32)
    return (grad_rows, grad_down, grad_up)


def solution(mesh):
    placed = (
        P(("groups", "job"), None, "tensor"),
        P(("groups", "job"), "tensor", None),
        P("tensor", None),
        P(("groups", "job"), "tensor", None),
        P(("groups", "job"), "tensor", None),
        P(("groups", "job"), None),
        P(("groups", "job"), None),
        P("groups"),
        P("groups"),
    )
    small = mesh.shape["job"] == JOBS and mesh.shape["tensor"] == 4
    return jax.shard_map(
        on_device if small else on_any_device,
        mesh=mesh,
        in_specs=placed,
        out_specs=(
            P(("groups", "job"), None, "tensor"),
            P(("groups", "job"), "tensor", None),
            P(("groups", "job"), "tensor", None),
        ),
        check_vma=False,
    )
```

```python
import functools
import math

import jax
import jax.numpy as jnp
from jax import lax
from jax.experimental import pallas as pl
from jax.experimental.pallas import tpu as pltpu
from jax.sharding import PartitionSpec as P

F32 = jnp.float32
BF16 = jnp.bfloat16
VMEM_LIMIT = 28 * 1024 * 1024
CHUNKS = 5
JOBS = 4
PAIR = [(0, 1), (1, 0), (2, 3), (3, 2)]
MIDDLE = [
    pair
    for t in range(4)
    for pair in ((t * 4 + 1, t * 4 + 2), (t * 4 + 2, t * 4 + 1), (t * 4, (t ^ 1) * 4), (t * 4 + 3, (t ^ 1) * 4 + 3))
]
TENSOR_X = [(0, 2), (2, 0), (1, 3), (3, 1)]
TENSOR_CORE = [(0, 1), (1, 0), (2, 3), (3, 2)]


def params():
    return pltpu.CompilerParams(vmem_limit_bytes=VMEM_LIMIT)


def cost(flops, moved):
    return pl.CostEstimate(flops=flops, bytes_accessed=moved, transcendentals=0)


def whole(shape):
    return pl.BlockSpec(shape, lambda *_: (0,) * len(shape))


def far(value):
    return pltpu.with_memory_space_constraint(value, pltpu.HBM)


def smem():
    return pl.BlockSpec(memory_space=pltpu.SMEM)


def turn_kernel(down_ref, low_ref, high_ref):
    turned = down_ref[...].T
    half = low_ref.shape[0]
    low_ref[...] = turned[:half]
    high_ref[...] = turned[half:]


def turn(down, tile):
    width, rank = down.shape
    half = rank // 2
    out = jax.ShapeDtypeStruct((half, width), down.dtype)
    return pl.pallas_call(
        turn_kernel,
        grid=(width // tile,),
        in_specs=[pl.BlockSpec((tile, rank), lambda i: (i, 0))],
        out_specs=[pl.BlockSpec((half, tile), lambda i: (0, i))] * 2,
        out_shape=[out, out],
        compiler_params=params(),
        cost_estimate=cost(0, 4 * width * rank),
        name="turn_adapter",
    )(down)


def block_factor(ids, lengths, owners, ranks, b, rows, width):
    adapter = ids[0, b]
    rank = ranks[adapter]
    live = lax.broadcasted_iota(jnp.int32, (rows, width), 0) < lengths[0, b]
    keep = lax.broadcasted_iota(jnp.int32, (rows, width), 1) < rank
    scale = jnp.float32(width) / (2.0 * rank.astype(F32))
    return owners[adapter], jnp.where(live & keep, scale, 0.0)


def spread(low, slot):
    half = low.shape[1] // 2
    lanes = lax.broadcasted_iota(jnp.int32, low.shape, 1)
    turned = pltpu.roll(low, half, 1)
    twice = jnp.where(lanes < half, low, turned)
    chunk = jnp.where(lanes < half, 0, 1)
    return jnp.concatenate(
        [
            jnp.where(chunk == slot, twice, 0.0),
            jnp.where(chunk + 2 == slot, twice, 0.0),
            jnp.where(lanes < half, turned, 0.0),
        ],
        axis=1,
    )


def gathered(full, slot, rank):
    half = rank // 2
    odd = lax.rem(slot, 2)
    both = jnp.where(slot >= 2, full[:, rank : 2 * rank], full[:, :rank])
    turned = pltpu.roll(both, half, 1)
    lower = jnp.where(odd == 1, turned, both)
    upper = pltpu.roll(full[:, 2 * rank :], half, 1)
    lanes = lax.broadcasted_iota(jnp.int32, both.shape, 1)
    return jnp.where(lanes < half, lower, upper)


def roles(z, excess):
    inner = (z == 1) | (z == 2)
    mine = jnp.where(z < 2, 1, 2)
    far_in = 3 - mine
    far_out = jnp.where(z < 2, 3, 0)
    top_in, top_far_in = excess == mine, excess == far_in
    spare = CHUNKS - 1
    return [
        jnp.where(
            inner, jnp.where(top_far_in, far_out, spare), jnp.where(top_in | top_far_in, far_out, spare)
        ),
        jnp.where(
            inner,
            jnp.where(top_far_in, spare, far_out),
            jnp.where(top_in, far_in, jnp.where(top_far_in, spare, far_out)),
        ),
        jnp.where(inner | top_in, spare, far_in),
        jnp.bitwise_xor(z, 1),
        far_in,
        z,
        jnp.int32(spare),
    ]


def pull_kernel(norm, ids, lengths, owners, ranks, place, g0, g1, g2, g3, u0, u1, u2, u3, x_ref, *rest):
    parts, (wide_ref, up, turned, sums) = rest[:7], rest[7:]
    t, z = place[0], place[1]
    quarter, values = g0.shape
    rank = u0.shape[2]
    half = rank // 2
    block = x_ref.shape[0] // ids.shape[1]

    @pl.when(pl.program_id(0) == 0)
    def _():
        for q, u in enumerate((u0, u1, u2, u3)):
            start = pl.multiple_of(jnp.bitwise_xor(t, q) * quarter, quarter)
            for d in range(JOBS):
                slot = jnp.bitwise_xor(z, d)
                up[slot, pl.ds(start, quarter), :] = u[d]
        for q, g in enumerate((g0, g1, g2, g3)):
            for j in range(quarter // block):
                b = jnp.bitwise_xor(t, q) * (quarter // block) + j
                slot, factor = block_factor(ids, lengths, owners, ranks, b, block, rank)
                pulled = jnp.dot(g[j * block : (j + 1) * block, :], up[slot], preferred_element_type=F32)
                low = spread((pulled * factor).astype(BF16).astype(F32), slot)
                rows = pl.ds(pl.multiple_of(b * block, block), block)
                wide_ref[rows, :] = low.astype(BF16)
                turned[:, rows] = low.T.astype(BF16)

    sums[...] = (
        jnp.dot(turned[: CHUNKS * half, :], x_ref[...], preferred_element_type=F32) * norm
    ).astype(BF16)
    for part, chunk in zip(parts, roles(z, place[2])):
        part[...] = sums[pl.ds(pl.multiple_of(chunk * half, half), half), :]


def pull(tables, place, grads, ups, features, norm, tile):
    rows, width = features.shape
    quarter, values = grads[0].shape
    rank = ups[0].shape[2]
    used = CHUNKS * rank // 2
    return pl.pallas_call(
        functools.partial(pull_kernel, norm),
        grid=(width // tile,),
        in_specs=[smem()] * 5
        + [whole((quarter, values))] * 4
        + [whole((JOBS, quarter, rank))] * 4
        + [pl.BlockSpec((rows, tile), lambda i: (0, i))],
        out_specs=[pl.BlockSpec((rank // 2, tile), lambda i: (0, i))] * 7 + [whole((rows, 3 * rank))],
        out_shape=[jax.ShapeDtypeStruct((rank // 2, width), BF16)] * 7
        + [jax.ShapeDtypeStruct((rows, 3 * rank), BF16)],
        scratch_shapes=[
            pltpu.VMEM((JOBS, values, rank), BF16),
            pltpu.VMEM((3 * rank, rows), BF16),
            pltpu.VMEM((used, tile), BF16),
        ],
        compiler_params=params(),
        cost_estimate=cost(2 * used * rows * width, 2 * (rows * width + used * width + 2 * rows * values)),
        name="pull_and_part_down",
    )(*tables, place, far(grads[0]), *grads[1:], *ups, far(features))


def arrivals(z, excess):
    inner = (z == 1) | (z == 2)
    mine = jnp.where(z < 2, 1, 2)
    outer = jnp.where(z < 2, 0, 3)
    far_in, far_out = 3 - mine, 3 - outer
    top_in, top_out = excess == mine, excess == outer
    top_far_in, top_far_out = excess == far_in, excess == far_out
    spare, none = CHUNKS - 1, CHUNKS + 1
    return [
        z,
        jnp.where(excess == z, spare, none),
        jnp.where(inner, outer, mine),
        jnp.where(inner, jnp.where(top_out, spare, none), jnp.where(top_in, spare, far_in)),
        jnp.where(inner, none, jnp.where(top_in, far_in, jnp.where(top_far_in, spare, far_out))),
        jnp.where(
            inner, none, jnp.where(top_in | top_far_in, far_out, jnp.where(top_far_out, spare, none))
        ),
        jnp.where(inner, far_in, none),
        jnp.where(inner, jnp.where(top_far_in, spare, far_out), none),
        jnp.where(
            inner, jnp.where(top_far_in, far_out, jnp.where(top_far_out, spare, none)), none
        ),
    ]


def project_kernel(ids, owners, place, *refs):
    chunks = refs[:9]
    x_ref, out_ref, table_ref, turned, sems = refs[9:]
    half, width = chunks[0].shape
    rank = 2 * half
    rows = x_ref.shape[0]
    used = CHUNKS * half

    @pl.when(pl.program_id(0) == 0)
    def _():
        where_to = arrivals(place[1], place[2])

        def chunk_copy(k):
            start = pl.multiple_of(where_to[k] * half, half)
            return pltpu.make_async_copy(chunks[k], table_ref.at[pl.ds(start, half), :], sems.at[k])

        for k in range(9):
            pl.when(where_to[k] < CHUNKS)(chunk_copy(k).start)
        table_ref[used:, :] = jnp.zeros((half, width), BF16)
        for k in range(9):
            pl.when(where_to[k] < CHUNKS)(chunk_copy(k).wait)

    turned[...] = lax.dot_general(
        table_ref[:used, :], x_ref[...], (((1,), (1,)), ((), ())), preferred_element_type=F32
    )
    first = pl.program_id(0) * (rows // rank)
    for j in range(rows // rank):
        slot = owners[ids[0, first + j]]
        columns = slice(j * rank, (j + 1) * rank)
        piece = jnp.concatenate(
            [turned[pl.ds(pl.multiple_of(slot * half, half), half), columns], turned[used - half :, columns]], axis=0
        )
        out_ref[columns, :] = piece.T.astype(BF16)


def project(ids, owners, place, chunks, features, tile):
    rows, width = features.shape
    half = chunks[0].shape[0]
    return pl.pallas_call(
        project_kernel,
        grid=(rows // tile,),
        in_specs=[smem()] * 3
        + [pl.BlockSpec(memory_space=pl.ANY)] * 9
        + [pl.BlockSpec((tile, width), lambda i: (i, 0))],
        out_specs=[
            pl.BlockSpec((tile, 2 * half), lambda i: (i, 0)),
            whole((6 * half, width)),
        ],
        out_shape=[
            jax.ShapeDtypeStruct((rows, 2 * half), BF16),
            jax.ShapeDtypeStruct((6 * half, width), BF16),
        ],
        scratch_shapes=[pltpu.VMEM((CHUNKS * half, tile), F32), pltpu.SemaphoreType.DMA((9,))],
        compiler_params=params(),
        cost_estimate=cost(2 * 6 * half * rows * width, 2 * (rows * width + 12 * half * width)),
        name="project",
    )(ids, owners, place, *chunks, far(features))


def base_kernel(lengths, place, g0, g1, g2, g3, weight_ref, out_ref):
    t = place[0]
    quarter, values = g0.shape
    block = out_ref.shape[0] // lengths.shape[1]
    tile = out_ref.shape[1]
    for q, g in enumerate((g0, g1, g2, g3)):
        start = pl.multiple_of(jnp.bitwise_xor(t, q) * quarter, quarter)
        term = lax.dot_general(
            g[...], weight_ref[...], (((1,), (1,)), ((), ())), preferred_element_type=F32
        )
        for j in range(quarter // block):
            b = jnp.bitwise_xor(t, q) * (quarter // block) + j
            live = lax.broadcasted_iota(jnp.int32, (block, tile), 0) < lengths[0, b]
            out_ref[pl.ds(pl.multiple_of(start + j * block, block), block), :] = jnp.where(
                live, term[j * block : (j + 1) * block], 0.0
            ).astype(BF16)


def base(lengths, place, grads, weight, half_index, tile):
    width, values = weight.shape[0] // 2, weight.shape[1]
    quarter = grads[0].shape[0]
    rows = 4 * quarter
    first = half_index * (width // tile)
    return pl.pallas_call(
        base_kernel,
        grid=(width // tile,),
        in_specs=[smem()] * 2
        + [whole((quarter, values))] * 4
        + [pl.BlockSpec((tile, values), lambda i: (first + i, 0))],
        out_specs=pl.BlockSpec((rows, tile), lambda i: (0, i)),
        out_shape=jax.ShapeDtypeStruct((rows, width), BF16),
        compiler_params=params(),
        cost_estimate=cost(2 * rows * width * values, 2 * (rows * values + width * values + rows * width)),
        name="base_term",
    )(lengths, place, *map(far, grads), far(weight))


def rows_kernel(wide_ref, table_ref, base_ref, out_ref):
    out_ref[...] = (
        base_ref[...].astype(F32) + jnp.dot(wide_ref[...], table_ref[...], preferred_element_type=F32)
    ).astype(BF16)


def add_rows(wide, table, base_half, tile):
    rows, deep = wide.shape
    width = table.shape[1]
    return pl.pallas_call(
        rows_kernel,
        grid=(width // tile // 2,),
        in_specs=[
            whole((rows, deep)),
            pl.BlockSpec((deep, tile), lambda i: (0, i)),
            pl.BlockSpec((rows, tile), lambda i: (0, i)),
        ],
        out_specs=pl.BlockSpec((rows, tile), lambda i: (0, i)),
        out_shape=jax.ShapeDtypeStruct((rows, width), BF16),
        compiler_params=params(),
        cost_estimate=cost(rows * width * deep, 2 * (rows * width + deep * (rows + width // 2))),
        name="grad_rows",
    )(wide, table, base_half)


def part_up_kernel(norm, ids, lengths, owners, ranks, place, g0, g1, g2, g3, a_ref, b_ref, *rest):
    outs, (slice_ref, wide) = rest[:JOBS], rest[JOBS:]
    t, z, excess = place[0], place[1], place[2]
    quarter, values = g0.shape
    rank = a_ref.shape[1]
    half = rank // 2
    block = a_ref.shape[0] // ids.shape[1]
    columns = pl.ds(pl.multiple_of(t * quarter, quarter), quarter)
    for q, g in enumerate((g0, g1, g2, g3)):
        start = pl.multiple_of(jnp.bitwise_xor(t, q) * quarter, quarter)
        slice_ref[pl.ds(start, quarter), :] = g[:, columns]
    for b in range(ids.shape[1]):
        slot, factor = block_factor(ids, lengths, owners, ranks, b, block, rank)
        rows = slice(b * block, (b + 1) * block)
        low = (a_ref[rows, :].astype(F32) + b_ref[rows, :].astype(F32)) * factor
        wide[rows, :] = spread(low.astype(BF16).astype(F32), slot).astype(BF16)
    full = (
        lax.dot_general(slice_ref[...], wide[...], (((0,), (0,)), ((), ())), preferred_element_type=F32) * norm
    )
    lanes = lax.broadcasted_iota(jnp.int32, (quarter, rank), 1)
    for d, out in enumerate(outs):
        slot = jnp.bitwise_xor(z, d)
        keep = jnp.where(slot == excess, rank, half)
        out[...] = jnp.where(lanes < keep, gathered(full, slot, rank), 0.0).astype(BF16)


def part_up(tables, place, grads, sums, norm):
    quarter, values = grads[0].shape
    rows, rank = sums[0].shape
    vmem = pl.BlockSpec(memory_space=pltpu.VMEM)
    return pl.pallas_call(
        functools.partial(part_up_kernel, norm),
        in_specs=[smem()] * 5 + [vmem] * 6,
        out_specs=[vmem] * JOBS,
        out_shape=[jax.ShapeDtypeStruct((quarter, rank), BF16)] * JOBS,
        scratch_shapes=[
            pltpu.VMEM((rows, quarter), BF16),
            pltpu.VMEM((rows, 3 * rank), BF16),
        ],
        compiler_params=params(),
        cost_estimate=cost(2 * rows * quarter * 3 * rank, 2 * (rows * values + 2 * rows * rank)),
        name="part_up",
    )(*tables, place, *grads, *sums)


def last_kernel(place, wide_ref, table_ref, base_ref, own0, own1, t1, n1, t2, n2, filled_ref, rows_ref, down_ref):
    del filled_ref
    half = own0.shape[0]
    rank = 2 * half
    total = (
        jnp.concatenate([own0[...], own1[...]], axis=0).astype(F32)
        + jnp.concatenate([t1[...], t2[...]], axis=0).astype(F32)
    )
    inner = (place[1] == 1) | (place[1] == 2)
    total += jnp.where(inner, jnp.concatenate([n1[...], n2[...]], axis=0).astype(F32), 0.0)
    keep = jnp.where(place[1] == place[2], rank, half)
    rows = lax.broadcasted_iota(jnp.int32, total.shape, 0)
    down_ref[...] = jnp.where(rows < keep, total, 0.0).T
    rows_ref[...] = (
        base_ref[...].astype(F32) + jnp.dot(wide_ref[...], table_ref[...], preferred_element_type=F32)
    ).astype(BF16)


def last(place, wide, table, base_half, filled, sums, steps):
    rows, deep = wide.shape
    half, width = sums[0].shape
    tile, piece = width // 2 // steps, width // steps
    return pl.pallas_call(
        last_kernel,
        grid=(steps,),
        in_specs=[
            smem(),
            whole((rows, deep)),
            pl.BlockSpec((deep, tile), lambda i: (0, steps + i)),
            pl.BlockSpec((rows, tile), lambda i: (0, i)),
        ]
        + [pl.BlockSpec((half, piece), lambda i: (0, i))] * 6
        + [pl.BlockSpec(memory_space=pl.ANY)],
        out_specs=[
            pl.BlockSpec((rows, tile), lambda i: (0, steps + i)),
            pl.BlockSpec((piece, 2 * half), lambda i: (i, 0)),
        ],
        out_shape=[
            jax.ShapeDtypeStruct((rows, width), BF16),
            jax.ShapeDtypeStruct((width, 2 * half), F32),
        ],
        input_output_aliases={10: 0},
        compiler_params=params(),
        cost_estimate=cost(rows * width * deep, 2 * (rows * width + deep * (rows + width // 2) + 10 * half * width)),
        name="grad_rows_and_down",
    )(place, wide, table, base_half, *sums, filled)


def on_device(
    inputs,
    grad_out,
    value_weight,
    adapter_down,
    adapter_up,
    block_adapter,
    block_length,
    owner_slot,
    adapter_rank,
):
    features = inputs[0]
    row_count, local_width = features.shape
    half = adapter_down.shape[2] // 2
    tile = 512
    norm = 1.0 / math.sqrt(JOBS * row_count)
    t, z = lax.axis_index("tensor"), lax.axis_index("job")
    excess = jnp.sum(jnp.where(adapter_rank > half, owner_slot, 0)).astype(jnp.int32)
    place = jnp.stack([t, z, excess]).astype(jnp.int32)
    tables = (block_adapter, block_length, owner_slot, adapter_rank)

    inner = (z == 1) | (z == 2)
    mine = jnp.where(z < 2, 1, 2)
    top_in = excess == mine

    pair = lambda value: lax.ppermute(value, "job", PAIR)
    middle = lambda value: lax.ppermute(value, ("tensor", "job"), MIDDLE)
    swap = lambda value, d: lax.ppermute(value, "job", [(i, i ^ d) for i in range(JOBS)])
    across = lambda value: lax.ppermute(value, "tensor", TENSOR_X)
    beside = lambda value: lax.ppermute(value, "tensor", TENSOR_CORE)

    tie = lax.optimization_barrier

    up = adapter_up[0]
    g0 = grad_out[0]
    g2 = across(g0)
    g1 = beside(g0)
    up_z = jnp.stack([up] + [swap(up, d) for d in (1, 2, 3)])
    up_x = across(up_z)

    low, high = turn(adapter_down[0], local_width)
    s1 = pair(low)
    m1 = middle(low)

    up_x, g2, g1, up_z = tie((up_x, g2, g1, up_z))
    to_c = jnp.stack([up_z, up_x])
    g3 = beside(g2)
    up_c = beside(to_c)
    s1, m1, to_c = tie((s1, m1, to_c))
    to_s2 = jnp.where(inner & ~top_in, m1, high)
    to_m2 = jnp.where(top_in, high, s1)
    s2 = pair(to_s2)
    m2 = middle(to_m2)

    to_s2, to_m2, up_c, g3 = tie((to_s2, to_m2, up_c, g3))
    grads = (g0, g1, g2, g3)
    ups = (up_z, up_c[0], up_x, up_c[1])
    *parts, wide = pull(tables, place, grads, ups, features, norm, 1024)

    def added(part, value, use=None):
        value = value.astype(F32)
        return (part.astype(F32) + (value if use is None else jnp.where(use, value, 0.0))).astype(BF16)

    *parts, s2, m2 = tie((*parts, s2, m2))
    to_s3 = jnp.where(inner, jnp.where(top_in, m1, m2), parts[0])
    to_m3 = jnp.where(top_in, s1, s2)
    to_s3, to_m3, *grads = tie((to_s3, to_m3, *grads))
    s3 = pair(to_s3)
    m3 = middle(to_m3)
    base_a = base(block_length, place, grads, value_weight, 0, 768)
    s3, m3, base_a = tie((s3, m3, base_a))
    to_s4 = jnp.where(inner, jnp.where(top_in, m2, m3), parts[1])
    to_n3 = added(parts[0], s3, ~top_in)
    to_s4, to_n3, *grads = tie((to_s4, to_n3, *grads))
    s4 = pair(to_s4)
    n3 = middle(to_n3)
    base_b = base(block_length, place, grads, value_weight, 1, 768)
    s4, n3, base_b = tie((s4, n3, base_b))

    to_s5 = added(parts[2], n3, inner & ~top_in)
    to_n2 = added(parts[1], jnp.where(top_in, s3, s4))
    to_s5, to_n2, to_project = tie((to_s5, to_n2, s4))
    s5 = pair(to_s5)
    n2 = middle(to_n2)
    partial, table = project(
        block_adapter, owner_slot, place, (low, high, s1, s2, s3, to_project, m1, m2, m3), features, 512
    )
    partial, s5, n2 = tie((partial, s5, n2))
    beyond = across(partial)
    to_s6 = added(parts[3], jnp.where(top_in, n3, n2), inner)
    to_n1 = added(parts[4], jnp.where(top_in, s4, s5))
    to_s6, to_n1, wide, table, base_a, base_b = tie((to_s6, to_n1, wide, table, base_a, base_b))
    s6 = pair(to_s6)
    n1 = middle(to_n1)
    grad_rows = add_rows(wide, table, base_a, 768)
    grad_rows, beyond = tie((grad_rows, beyond))
    both = (partial.astype(F32) + beyond.astype(F32)).astype(BF16)
    other = beside(both)

    ours = part_up(tables, place, grads, (both, other), norm)
    theirs = [swap(ours[d], d) for d in (1, 2, 3)]
    wide, table, base_b, _ = tie((wide, table, base_b, ours[1]))
    grad_rows, grad_down = last(place, wide, table, base_b, grad_rows, (parts[5], parts[6], s6, n1, s5, n2), 4)
    grad_rows, grad_down, *theirs = tie((grad_rows, grad_down, *theirs))
    grad_up = ours[0].astype(F32)
    for value in theirs:
        grad_up = grad_up + value.astype(F32)
    return (grad_rows[None], grad_down[None], grad_up[None])


def block_tables(block_ids, block_sizes, owner_slot, adapter_rank, block_rows, rank_width):
    adapter_count = owner_slot.shape[0]
    matches = (block_ids[:, None] == jnp.arange(adapter_count, dtype=jnp.int32)[None, :]).astype(
        jnp.int32
    )
    slot_index = jnp.sum(matches * owner_slot[None, :], axis=1)
    rank_used = jnp.sum(matches * adapter_rank[None, :], axis=1)
    selector = (slot_index[:, None] == jnp.arange(adapter_count, dtype=jnp.int32)[None, :]).astype(F32)
    live_rows = (jnp.arange(block_rows, dtype=jnp.int32)[None, :] < block_sizes[:, None]).astype(F32)
    keep_ranks = (jnp.arange(rank_width, dtype=jnp.int32)[None, :] < rank_used[:, None]).astype(F32)
    scaling = rank_width / (2.0 * rank_used.astype(F32))
    factor = live_rows[:, :, None] * keep_ranks[:, None, :] * scaling[:, None, None]
    return (slot_index, selector, live_rows, factor)


def on_any_device(
    inputs,
    grad_out,
    value_weight,
    adapter_down,
    adapter_up,
    block_adapter,
    block_length,
    owner_slot,
    adapter_rank,
):
    highest = lax.Precision.HIGHEST
    features = inputs[0]
    row_count, local_width = features.shape
    block_count = block_adapter.shape[1]
    block_rows = row_count // block_count
    rank_width = adapter_down.shape[2]
    local_values = adapter_up.shape[1]
    norm = 1.0 / math.sqrt(lax.axis_size("job") * row_count)
    cotangent = lax.all_gather(grad_out, "tensor", axis=1, tiled=True)[0]
    slot_index, selector, live_rows, factor = block_tables(
        block_adapter[0], block_length[0], owner_slot, adapter_rank, block_rows, rank_width
    )
    base_term = lax.dot_general(
        cotangent, value_weight, (((1,), (1,)), ((), ())), preferred_element_type=F32
    )
    value_start = lax.axis_index("tensor") * local_values
    cot_slice = lax.dynamic_slice_in_dim(cotangent, value_start, local_values, 1).reshape(
        block_count, block_rows, local_values
    )
    feat_blocks = features.reshape(block_count, block_rows, local_width)
    down_all = lax.all_gather(adapter_down, "job", axis=0, tiled=True)
    up_all = lax.all_gather(adapter_up, "job", axis=0, tiled=True)
    down_used = jnp.take(down_all, slot_index, axis=0)
    up_used = jnp.take(up_all, slot_index, axis=0)
    projected = jnp.einsum("btd,bdr->btr", feat_blocks, down_used, preferred_element_type=F32)
    pulled = jnp.einsum("btk,bkr->btr", cot_slice, up_used, preferred_element_type=F32)
    projected = lax.psum(projected.astype(BF16), "tensor").astype(F32)
    pulled = lax.psum(pulled.astype(BF16), "tensor").astype(F32)
    low_down = (projected * factor).astype(BF16)
    low_grad = (pulled * factor).astype(BF16)
    adapter_term = jnp.einsum(
        "btr,bdr->btd", low_grad, down_used, preferred_element_type=F32
    ).reshape(row_count, local_width)
    grad_rows = (base_term * live_rows.reshape(row_count)[:, None] + adapter_term).astype(BF16)[None]
    block_down = jnp.einsum("btd,btr->bdr", feat_blocks, low_grad, preferred_element_type=F32)
    block_up = jnp.einsum("btk,btr->bkr", cot_slice, low_down, preferred_element_type=F32)
    part_down = jnp.einsum("bs,bdr->sdr", selector, block_down, precision=highest) * norm
    part_up_sum = jnp.einsum("bs,bkr->skr", selector, block_up, precision=highest) * norm
    grad_down = lax.psum_scatter(part_down.astype(BF16), "job", scatter_dimension=0, tiled=True).astype(F32)
    grad_up = lax.psum_scatter(part_up_sum.astype(BF16), "job", scatter_dimension=0, tiled=True).astype(F32)
    return (grad_rows, grad_down, grad_up)


def solution(mesh):
    placed = (
        P(("groups", "job"), None, "tensor"),
        P(("groups", "job"), "tensor", None),
        P("tensor", None),
        P(("groups", "job"), "tensor", None),
        P(("groups", "job"), "tensor", None),
        P(("groups", "job"), None),
        P(("groups", "job"), None),
        P("groups"),
        P("groups"),
    )
    small = mesh.shape["job"] == JOBS and mesh.shape["tensor"] == 4
    return jax.shard_map(
        on_device if small else on_any_device,
        mesh=mesh,
        in_specs=placed,
        out_specs=(
            P(("groups", "job"), None, "tensor"),
            P(("groups", "job"), "tensor", None),
            P(("groups", "job"), "tensor", None),
        ),
        check_vma=False,
    )
```

```python
import functools
import math

import jax
import jax.numpy as jnp
from jax import lax
from jax.experimental import pallas as pl
from jax.experimental.pallas import tpu as pltpu
from jax.sharding import PartitionSpec as P

F32 = jnp.float32
BF16 = jnp.bfloat16
VMEM_LIMIT = 28 * 1024 * 1024
CHUNKS = 5
JOBS = 4
PAIR = [(0, 1), (1, 0), (2, 3), (3, 2)]
MIDDLE = [
    pair
    for t in range(4)
    for pair in ((t * 4 + 1, t * 4 + 2), (t * 4 + 2, t * 4 + 1), (t * 4, (t ^ 1) * 4), (t * 4 + 3, (t ^ 1) * 4 + 3))
]
TENSOR_X = [(0, 2), (2, 0), (1, 3), (3, 1)]
TENSOR_CORE = [(0, 1), (1, 0), (2, 3), (3, 2)]


def params():
    return pltpu.CompilerParams(vmem_limit_bytes=VMEM_LIMIT)


def cost(flops, moved):
    return pl.CostEstimate(flops=flops, bytes_accessed=moved, transcendentals=0)


def whole(shape):
    return pl.BlockSpec(shape, lambda *_: (0,) * len(shape))


def far(value):
    return pltpu.with_memory_space_constraint(value, pltpu.HBM)


def smem():
    return pl.BlockSpec(memory_space=pltpu.SMEM)


def turn_kernel(down_ref, low_ref, high_ref):
    turned = down_ref[...].T
    half = low_ref.shape[0]
    low_ref[...] = turned[:half]
    high_ref[...] = turned[half:]


def turn(down, tile):
    width, rank = down.shape
    half = rank // 2
    out = jax.ShapeDtypeStruct((half, width), down.dtype)
    return pl.pallas_call(
        turn_kernel,
        grid=(width // tile,),
        in_specs=[pl.BlockSpec((tile, rank), lambda i: (i, 0))],
        out_specs=[pl.BlockSpec((half, tile), lambda i: (0, i))] * 2,
        out_shape=[out, out],
        compiler_params=params(),
        cost_estimate=cost(0, 4 * width * rank),
        name="turn_adapter",
    )(down)


class Info:
    def __init__(self, ref):
        self.ref = ref
        self.blocks = (ref.shape[0] - 3 - 2 * JOBS) // 2

    @staticmethod
    def pack(ids, lengths, owners, ranks, place):
        return jnp.concatenate([ids[0], lengths[0], owners, ranks, place])

    def adapter(self, b):
        return self.ref[b]

    def length(self, b):
        return self.ref[self.blocks + b]

    def owner(self, adapter):
        return self.ref[2 * self.blocks + adapter]

    def rank(self, adapter):
        return self.ref[2 * self.blocks + JOBS + adapter]

    def place(self):
        first = 2 * self.blocks + 2 * JOBS
        return self.ref[first], self.ref[first + 1], self.ref[first + 2]


def block_factor(info, b, rows, width):
    adapter = info.adapter(b)
    rank = info.rank(adapter)
    live = lax.broadcasted_iota(jnp.int32, (rows, width), 0) < info.length(b)
    keep = lax.broadcasted_iota(jnp.int32, (rows, width), 1) < rank
    scale = jnp.float32(width) / (2.0 * rank.astype(F32))
    return info.owner(adapter), jnp.where(live & keep, scale, 0.0)


def spread(low, slot):
    half = low.shape[1] // 2
    lanes = lax.broadcasted_iota(jnp.int32, low.shape, 1)
    turned = pltpu.roll(low, half, 1)
    twice = jnp.where(lanes < half, low, turned)
    chunk = jnp.where(lanes < half, 0, 1)
    return jnp.concatenate(
        [
            jnp.where(chunk == slot, twice, 0.0),
            jnp.where(chunk + 2 == slot, twice, 0.0),
            jnp.where(lanes < half, turned, 0.0),
        ],
        axis=1,
    )


def gathered(full, slot, rank):
    half = rank // 2
    odd = lax.rem(slot, 2)
    both = jnp.where(slot >= 2, full[:, rank : 2 * rank], full[:, :rank])
    turned = pltpu.roll(both, half, 1)
    lower = jnp.where(odd == 1, turned, both)
    upper = pltpu.roll(full[:, 2 * rank :], half, 1)
    lanes = lax.broadcasted_iota(jnp.int32, both.shape, 1)
    return jnp.where(lanes < half, lower, upper)


def roles(z, excess):
    inner = (z == 1) | (z == 2)
    mine = jnp.where(z < 2, 1, 2)
    far_in = 3 - mine
    far_out = jnp.where(z < 2, 3, 0)
    top_in, top_far_in = excess == mine, excess == far_in
    spare = CHUNKS - 1
    return [
        jnp.where(
            inner, jnp.where(top_far_in, far_out, spare), jnp.where(top_in | top_far_in, far_out, spare)
        ),
        jnp.where(
            inner,
            jnp.where(top_far_in, spare, far_out),
            jnp.where(top_in, far_in, jnp.where(top_far_in, spare, far_out)),
        ),
        jnp.where(inner | top_in, spare, far_in),
        jnp.bitwise_xor(z, 1),
        far_in,
        z,
        jnp.int32(spare),
    ]


def pull_kernel(norm, info, g0, g1, g2, g3, z_ref, x_up_ref, core_ref, x_ref, *rest):
    u0, u2, (u1, u3) = z_ref, x_up_ref, (core_ref.at[0], core_ref.at[1])
    parts, (wide_ref, up, turned, sums) = rest[:7], rest[7:]
    info = Info(info)
    t, z, excess = info.place()
    quarter, values = g0.shape
    rank = up.shape[2]
    half = rank // 2
    block = x_ref.shape[0] // info.blocks

    @pl.when(pl.program_id(0) == 0)
    def _():
        for q, u in enumerate((u0, u1, u2, u3)):
            start = pl.multiple_of(jnp.bitwise_xor(t, q) * quarter, quarter)
            for d in range(JOBS):
                slot = jnp.bitwise_xor(z, d)
                up[slot, pl.ds(start, quarter), :] = u[d]
        for q, g in enumerate((g0, g1, g2, g3)):
            for j in range(quarter // block):
                b = jnp.bitwise_xor(t, q) * (quarter // block) + j
                slot, factor = block_factor(info, b, block, rank)
                pulled = jnp.dot(g[j * block : (j + 1) * block, :], up[slot], preferred_element_type=F32)
                low = spread((pulled * factor).astype(BF16).astype(F32), slot)
                rows = pl.ds(pl.multiple_of(b * block, block), block)
                wide_ref[rows, :] = low.astype(BF16)
                turned[:, rows] = low.T.astype(BF16)

    sums[...] = (
        jnp.dot(turned[: CHUNKS * half, :], x_ref[...], preferred_element_type=F32) * norm
    ).astype(BF16)
    for part, chunk in zip(parts, roles(z, excess)):
        part[...] = sums[pl.ds(pl.multiple_of(chunk * half, half), half), :]


def pull(info, grads, ups, features, norm, tile):
    rows, width = features.shape
    quarter, values = grads[0].shape
    rank = ups[0].shape[2]
    used = CHUNKS * rank // 2
    return pl.pallas_call(
        functools.partial(pull_kernel, norm),
        grid=(width // tile,),
        in_specs=[smem()]
        + [whole((quarter, values))] * 4
        + [whole((JOBS, quarter, rank))] * 2
        + [whole((2, JOBS, quarter, rank))]
        + [pl.BlockSpec((rows, tile), lambda i: (0, i))],
        out_specs=[pl.BlockSpec((rank // 2, tile), lambda i: (0, i))] * 7 + [whole((rows, 3 * rank))],
        out_shape=[jax.ShapeDtypeStruct((rank // 2, width), BF16)] * 7
        + [jax.ShapeDtypeStruct((rows, 3 * rank), BF16)],
        scratch_shapes=[
            pltpu.VMEM((JOBS, values, rank), BF16),
            pltpu.VMEM((3 * rank, rows), BF16),
            pltpu.VMEM((used, tile), BF16),
        ],
        compiler_params=params(),
        cost_estimate=cost(2 * used * rows * width, 2 * (rows * width + used * width + 2 * rows * values)),
        name="pull_and_part_down",
    )(info, far(grads[0]), *grads[1:], *ups, far(features))


def arrivals(z, excess):
    inner = (z == 1) | (z == 2)
    mine = jnp.where(z < 2, 1, 2)
    outer = jnp.where(z < 2, 0, 3)
    far_in, far_out = 3 - mine, 3 - outer
    top_in, top_out = excess == mine, excess == outer
    top_far_in, top_far_out = excess == far_in, excess == far_out
    spare, none = CHUNKS - 1, CHUNKS + 1
    return [
        z,
        jnp.where(excess == z, spare, none),
        jnp.where(inner, outer, mine),
        jnp.where(inner, jnp.where(top_out, spare, none), jnp.where(top_in, spare, far_in)),
        jnp.where(inner, none, jnp.where(top_in, far_in, jnp.where(top_far_in, spare, far_out))),
        jnp.where(
            inner, none, jnp.where(top_in | top_far_in, far_out, jnp.where(top_far_out, spare, none))
        ),
        jnp.where(inner, far_in, none),
        jnp.where(inner, jnp.where(top_far_in, spare, far_out), none),
        jnp.where(
            inner, jnp.where(top_far_in, far_out, jnp.where(top_far_out, spare, none)), none
        ),
    ]


def project_kernel(info, *refs):
    chunks = refs[:9]
    x_ref, out_ref, table_ref, turned, sems = refs[9:]
    info = Info(info)
    half, width = chunks[0].shape
    rank = 2 * half
    rows = x_ref.shape[0]
    used = CHUNKS * half

    @pl.when(pl.program_id(0) == 0)
    def _():
        _, z, excess = info.place()
        where_to = arrivals(z, excess)

        def chunk_copy(k):
            start = pl.multiple_of(where_to[k] * half, half)
            return pltpu.make_async_copy(chunks[k], table_ref.at[pl.ds(start, half), :], sems.at[k])

        for k in range(9):
            pl.when(where_to[k] < CHUNKS)(lambda k=k: chunk_copy(k).start())
        table_ref[used:, :] = jnp.zeros((half, width), BF16)
        for k in range(9):
            pl.when(where_to[k] < CHUNKS)(lambda k=k: chunk_copy(k).wait())

    turned[...] = lax.dot_general(
        table_ref[:used, :], x_ref[...], (((1,), (1,)), ((), ())), preferred_element_type=F32
    )
    first = pl.program_id(0) * (rows // rank)
    for j in range(rows // rank):
        slot = info.owner(info.adapter(first + j))
        columns = slice(j * rank, (j + 1) * rank)
        piece = jnp.concatenate(
            [turned[pl.ds(pl.multiple_of(slot * half, half), half), columns], turned[used - half :, columns]], axis=0
        )
        out_ref[columns, :] = piece.T.astype(BF16)


def project(info, chunks, features, tile):
    rows, width = features.shape
    half = chunks[0].shape[0]
    return pl.pallas_call(
        project_kernel,
        grid=(rows // tile,),
        in_specs=[smem()]
        + [pl.BlockSpec(memory_space=pl.ANY)] * 9
        + [pl.BlockSpec((tile, width), lambda i: (i, 0))],
        out_specs=[
            pl.BlockSpec((tile, 2 * half), lambda i: (i, 0)),
            whole((6 * half, width)),
        ],
        out_shape=[
            jax.ShapeDtypeStruct((rows, 2 * half), BF16),
            jax.ShapeDtypeStruct((6 * half, width), BF16),
        ],
        scratch_shapes=[pltpu.VMEM((CHUNKS * half, tile), F32), pltpu.SemaphoreType.DMA((9,))],
        compiler_params=params(),
        cost_estimate=cost(2 * 6 * half * rows * width, 2 * (rows * width + 12 * half * width)),
        name="project",
    )(info, *chunks, far(features))


def base_kernel(info, g0, g1, g2, g3, weight_ref, out_ref):
    info = Info(info)
    t, _, _ = info.place()
    quarter, values = g0.shape
    block = out_ref.shape[0] // info.blocks
    tile = out_ref.shape[1]
    for q, g in enumerate((g0, g1, g2, g3)):
        start = pl.multiple_of(jnp.bitwise_xor(t, q) * quarter, quarter)
        term = lax.dot_general(
            g[...], weight_ref[...], (((1,), (1,)), ((), ())), preferred_element_type=F32
        )
        for j in range(quarter // block):
            b = jnp.bitwise_xor(t, q) * (quarter // block) + j
            live = lax.broadcasted_iota(jnp.int32, (block, tile), 0) < info.length(b)
            out_ref[pl.ds(pl.multiple_of(start + j * block, block), block), :] = jnp.where(
                live, term[j * block : (j + 1) * block], 0.0
            ).astype(BF16)


def base(info, grads, weight, half_index, tile):
    width, values = weight.shape[0] // 2, weight.shape[1]
    quarter = grads[0].shape[0]
    rows = 4 * quarter
    first = half_index * (width // tile)
    return pl.pallas_call(
        base_kernel,
        grid=(width // tile,),
        in_specs=[smem()]
        + [whole((quarter, values))] * 4
        + [pl.BlockSpec((tile, values), lambda i: (first + i, 0))],
        out_specs=pl.BlockSpec((rows, tile), lambda i: (0, i)),
        out_shape=jax.ShapeDtypeStruct((rows, width), BF16),
        compiler_params=params(),
        cost_estimate=cost(2 * rows * width * values, 2 * (rows * values + width * values + rows * width)),
        name="base_term",
    )(info, *map(far, grads), far(weight))


def rows_kernel(wide_ref, table_ref, base_ref, out_ref):
    out_ref[...] = (
        base_ref[...].astype(F32) + jnp.dot(wide_ref[...], table_ref[...], preferred_element_type=F32)
    ).astype(BF16)


def add_rows(wide, table, base_half, tile):
    rows, deep = wide.shape
    width = table.shape[1]
    return pl.pallas_call(
        rows_kernel,
        grid=(width // tile // 2,),
        in_specs=[
            whole((rows, deep)),
            pl.BlockSpec((deep, tile), lambda i: (0, i)),
            pl.BlockSpec((rows, tile), lambda i: (0, i)),
        ],
        out_specs=pl.BlockSpec((rows, tile), lambda i: (0, i)),
        out_shape=jax.ShapeDtypeStruct((rows, width), BF16),
        compiler_params=params(),
        cost_estimate=cost(rows * width * deep, 2 * (rows * width + deep * (rows + width // 2))),
        name="grad_rows",
    )(wide, table, base_half)


def part_up_kernel(norm, info, g0, g1, g2, g3, a_ref, b_ref, *rest):
    outs, (slice_ref, wide) = rest[:JOBS], rest[JOBS:]
    info = Info(info)
    t, z, excess = info.place()
    quarter, values = g0.shape
    rank = a_ref.shape[1]
    half = rank // 2
    block = a_ref.shape[0] // info.blocks
    columns = pl.ds(pl.multiple_of(t * quarter, quarter), quarter)
    for q, g in enumerate((g0, g1, g2, g3)):
        start = pl.multiple_of(jnp.bitwise_xor(t, q) * quarter, quarter)
        slice_ref[pl.ds(start, quarter), :] = g[:, columns]
    for b in range(info.blocks):
        slot, factor = block_factor(info, b, block, rank)
        rows = slice(b * block, (b + 1) * block)
        low = (a_ref[rows, :].astype(F32) + b_ref[rows, :].astype(F32)) * factor
        wide[rows, :] = spread(low.astype(BF16).astype(F32), slot).astype(BF16)
    full = (
        lax.dot_general(slice_ref[...], wide[...], (((0,), (0,)), ((), ())), preferred_element_type=F32) * norm
    )
    lanes = lax.broadcasted_iota(jnp.int32, (quarter, rank), 1)
    for d, out in enumerate(outs):
        slot = jnp.bitwise_xor(z, d)
        keep = jnp.where(slot == excess, rank, half)
        out[...] = jnp.where(lanes < keep, gathered(full, slot, rank), 0.0).astype(BF16)


def part_up(info, grads, sums, norm):
    quarter, values = grads[0].shape
    rows, rank = sums[0].shape
    vmem = pl.BlockSpec(memory_space=pltpu.VMEM)
    return pl.pallas_call(
        functools.partial(part_up_kernel, norm),
        in_specs=[smem()] + [vmem] * 6,
        out_specs=[vmem] * JOBS,
        out_shape=[jax.ShapeDtypeStruct((quarter, rank), BF16)] * JOBS,
        scratch_shapes=[
            pltpu.VMEM((rows, quarter), BF16),
            pltpu.VMEM((rows, 3 * rank), BF16),
        ],
        compiler_params=params(),
        cost_estimate=cost(2 * rows * quarter * 3 * rank, 2 * (rows * values + 2 * rows * rank)),
        name="part_up",
    )(info, *grads, *sums)


def last_kernel(info, wide_ref, table_ref, base_ref, own0, own1, t1, n1, t2, n2, filled_ref, rows_ref, down_ref):
    del filled_ref
    _, z, excess = Info(info).place()
    half = own0.shape[0]
    rank = 2 * half
    total = (
        jnp.concatenate([own0[...], own1[...]], axis=0).astype(F32)
        + jnp.concatenate([t1[...], t2[...]], axis=0).astype(F32)
    )
    inner = (z == 1) | (z == 2)
    total += jnp.where(inner, jnp.concatenate([n1[...], n2[...]], axis=0).astype(F32), 0.0)
    keep = jnp.where(z == excess, rank, half)
    rows = lax.broadcasted_iota(jnp.int32, total.shape, 0)
    down_ref[...] = jnp.where(rows < keep, total, 0.0).T
    rows_ref[...] = (
        base_ref[...].astype(F32) + jnp.dot(wide_ref[...], table_ref[...], preferred_element_type=F32)
    ).astype(BF16)


def last(info, wide, table, base_half, filled, sums, steps):
    rows, deep = wide.shape
    half, width = sums[0].shape
    tile, piece = width // 2 // steps, width // steps
    return pl.pallas_call(
        last_kernel,
        grid=(steps,),
        in_specs=[
            smem(),
            whole((rows, deep)),
            pl.BlockSpec((deep, tile), lambda i: (0, steps + i)),
            pl.BlockSpec((rows, tile), lambda i: (0, i)),
        ]
        + [pl.BlockSpec((half, piece), lambda i: (0, i))] * 6
        + [pl.BlockSpec(memory_space=pl.ANY)],
        out_specs=[
            pl.BlockSpec((rows, tile), lambda i: (0, steps + i)),
            pl.BlockSpec((piece, 2 * half), lambda i: (i, 0)),
        ],
        out_shape=[
            jax.ShapeDtypeStruct((rows, width), BF16),
            jax.ShapeDtypeStruct((width, 2 * half), F32),
        ],
        input_output_aliases={10: 0},
        compiler_params=params(),
        cost_estimate=cost(rows * width * deep, 2 * (rows * width + deep * (rows + width // 2) + 10 * half * width)),
        name="grad_rows_and_down",
    )(info, wide, table, base_half, *sums, filled)


def on_device(
    inputs,
    grad_out,
    value_weight,
    adapter_down,
    adapter_up,
    block_adapter,
    block_length,
    owner_slot,
    adapter_rank,
):
    features = inputs[0]
    row_count, local_width = features.shape
    half = adapter_down.shape[2] // 2
    tile = 512
    norm = 1.0 / math.sqrt(JOBS * row_count)
    t, z = lax.axis_index("tensor"), lax.axis_index("job")
    excess = jnp.sum(jnp.where(adapter_rank > half, owner_slot, 0)).astype(jnp.int32)
    place = jnp.stack([t, z, excess]).astype(jnp.int32)
    info = Info.pack(block_adapter, block_length, owner_slot, adapter_rank, place)

    inner = (z == 1) | (z == 2)
    mine = jnp.where(z < 2, 1, 2)
    top_in = excess == mine

    pair = lambda value: lax.ppermute(value, "job", PAIR)
    middle = lambda value: lax.ppermute(value, ("tensor", "job"), MIDDLE)
    swap = lambda value, d: lax.ppermute(value, "job", [(i, i ^ d) for i in range(JOBS)])
    across = lambda value: lax.ppermute(value, "tensor", TENSOR_X)
    beside = lambda value: lax.ppermute(value, "tensor", TENSOR_CORE)

    tie = lax.optimization_barrier

    up = adapter_up[0]
    g0 = grad_out[0]
    g2 = across(g0)
    g1 = beside(g0)
    up_z = jnp.stack([up] + [swap(up, d) for d in (1, 2, 3)])
    up_x = across(up_z)

    low, high = turn(adapter_down[0], local_width)
    s1 = pair(low)
    m1 = middle(low)

    up_x, g2, g1, up_z = tie((up_x, g2, g1, up_z))
    to_c = jnp.stack([up_z, up_x])
    s1, m1, to_c, info = tie((s1, m1, to_c, info))
    to_s2 = jnp.where(inner & ~top_in, m1, high)
    to_m2 = jnp.where(top_in, high, s1)
    to_s2, to_m2, to_c, g2 = tie((to_s2, to_m2, to_c, g2))
    s2 = pair(to_s2)
    m2 = middle(to_m2)
    g3 = beside(g2)
    up_c = beside(to_c)

    to_s2, to_m2, up_c, g3 = tie((to_s2, to_m2, up_c, g3))
    grads = (g0, g1, g2, g3)
    ups = (up_z, up_x, up_c)
    *parts, wide = pull(info, grads, ups, features, norm, 1024)

    def added(part, value, use=None):
        value = value.astype(F32)
        return (part.astype(F32) + (value if use is None else jnp.where(use, value, 0.0))).astype(BF16)

    *parts, s2, m2 = tie((*parts, s2, m2))
    to_s3 = jnp.where(inner, jnp.where(top_in, m1, m2), parts[0])
    to_m3 = jnp.where(top_in, s1, s2)
    to_s3, to_m3, *grads = tie((to_s3, to_m3, *grads))
    s3 = pair(to_s3)
    m3 = middle(to_m3)
    base_a = base(info, grads, value_weight, 0, 768)
    s3, m3, base_a = tie((s3, m3, base_a))
    to_s4 = jnp.where(inner, jnp.where(top_in, m2, m3), parts[1])
    to_n3 = added(parts[0], s3, ~top_in)
    to_s4, to_n3, *grads = tie((to_s4, to_n3, *grads))
    s4 = pair(to_s4)
    n3 = middle(to_n3)
    base_b = base(info, grads, value_weight, 1, 768)
    s4, n3, base_b = tie((s4, n3, base_b))

    to_s5 = added(parts[2], n3, inner & ~top_in)
    to_n2 = added(parts[1], jnp.where(top_in, s3, s4))
    to_s5, to_n2, to_project = tie((to_s5, to_n2, s4))
    s5 = pair(to_s5)
    n2 = middle(to_n2)
    partial, table = project(
        info, (low, high, s1, s2, s3, to_project, m1, m2, m3), features, 512
    )
    partial, s5, n2 = tie((partial, s5, n2))
    beyond = across(partial)
    to_s6 = added(parts[3], jnp.where(top_in, n3, n2), inner)
    to_n1 = added(parts[4], jnp.where(top_in, s4, s5))
    to_s6, to_n1, wide, table, base_a, base_b = tie((to_s6, to_n1, wide, table, base_a, base_b))
    s6 = pair(to_s6)
    n1 = middle(to_n1)
    grad_rows = add_rows(wide, table, base_a, 768)
    grad_rows, beyond = tie((grad_rows, beyond))
    both = (partial.astype(F32) + beyond.astype(F32)).astype(BF16)
    other = beside(both)

    ours = part_up(info, grads, (both, other), norm)
    theirs = [swap(ours[d], d) for d in (1, 2, 3)]
    wide, table, base_b, _ = tie((wide, table, base_b, ours[1]))
    grad_rows, grad_down = last(info, wide, table, base_b, grad_rows, (parts[5], parts[6], s6, n1, s5, n2), 4)
    grad_rows, grad_down, *theirs = tie((grad_rows, grad_down, *theirs))
    grad_up = ours[0].astype(F32)
    for value in theirs:
        grad_up = grad_up + value.astype(F32)
    return (grad_rows[None], grad_down[None], grad_up[None])


def block_tables(block_ids, block_sizes, owner_slot, adapter_rank, block_rows, rank_width):
    adapter_count = owner_slot.shape[0]
    matches = (block_ids[:, None] == jnp.arange(adapter_count, dtype=jnp.int32)[None, :]).astype(
        jnp.int32
    )
    slot_index = jnp.sum(matches * owner_slot[None, :], axis=1)
    rank_used = jnp.sum(matches * adapter_rank[None, :], axis=1)
    selector = (slot_index[:, None] == jnp.arange(adapter_count, dtype=jnp.int32)[None, :]).astype(F32)
    live_rows = (jnp.arange(block_rows, dtype=jnp.int32)[None, :] < block_sizes[:, None]).astype(F32)
    keep_ranks = (jnp.arange(rank_width, dtype=jnp.int32)[None, :] < rank_used[:, None]).astype(F32)
    scaling = rank_width / (2.0 * rank_used.astype(F32))
    factor = live_rows[:, :, None] * keep_ranks[:, None, :] * scaling[:, None, None]
    return (slot_index, selector, live_rows, factor)


def on_any_device(
    inputs,
    grad_out,
    value_weight,
    adapter_down,
    adapter_up,
    block_adapter,
    block_length,
    owner_slot,
    adapter_rank,
):
    highest = lax.Precision.HIGHEST
    features = inputs[0]
    row_count, local_width = features.shape
    block_count = block_adapter.shape[1]
    block_rows = row_count // block_count
    rank_width = adapter_down.shape[2]
    local_values = adapter_up.shape[1]
    norm = 1.0 / math.sqrt(lax.axis_size("job") * row_count)
    cotangent = lax.all_gather(grad_out, "tensor", axis=1, tiled=True)[0]
    slot_index, selector, live_rows, factor = block_tables(
        block_adapter[0], block_length[0], owner_slot, adapter_rank, block_rows, rank_width
    )
    base_term = lax.dot_general(
        cotangent, value_weight, (((1,), (1,)), ((), ())), preferred_element_type=F32
    )
    value_start = lax.axis_index("tensor") * local_values
    cot_slice = lax.dynamic_slice_in_dim(cotangent, value_start, local_values, 1).reshape(
        block_count, block_rows, local_values
    )
    feat_blocks = features.reshape(block_count, block_rows, local_width)
    down_all = lax.all_gather(adapter_down, "job", axis=0, tiled=True)
    up_all = lax.all_gather(adapter_up, "job", axis=0, tiled=True)
    down_used = jnp.take(down_all, slot_index, axis=0)
    up_used = jnp.take(up_all, slot_index, axis=0)
    projected = jnp.einsum("btd,bdr->btr", feat_blocks, down_used, preferred_element_type=F32)
    pulled = jnp.einsum("btk,bkr->btr", cot_slice, up_used, preferred_element_type=F32)
    projected = lax.psum(projected.astype(BF16), "tensor").astype(F32)
    pulled = lax.psum(pulled.astype(BF16), "tensor").astype(F32)
    low_down = (projected * factor).astype(BF16)
    low_grad = (pulled * factor).astype(BF16)
    adapter_term = jnp.einsum(
        "btr,bdr->btd", low_grad, down_used, preferred_element_type=F32
    ).reshape(row_count, local_width)
    grad_rows = (base_term * live_rows.reshape(row_count)[:, None] + adapter_term).astype(BF16)[None]
    block_down = jnp.einsum("btd,btr->bdr", feat_blocks, low_grad, preferred_element_type=F32)
    block_up = jnp.einsum("btk,btr->bkr", cot_slice, low_down, preferred_element_type=F32)
    part_down = jnp.einsum("bs,bdr->sdr", selector, block_down, precision=highest) * norm
    part_up_sum = jnp.einsum("bs,bkr->skr", selector, block_up, precision=highest) * norm
    grad_down = lax.psum_scatter(part_down.astype(BF16), "job", scatter_dimension=0, tiled=True).astype(F32)
    grad_up = lax.psum_scatter(part_up_sum.astype(BF16), "job", scatter_dimension=0, tiled=True).astype(F32)
    return (grad_rows, grad_down, grad_up)


def solution(mesh):
    placed = (
        P(("groups", "job"), None, "tensor"),
        P(("groups", "job"), "tensor", None),
        P("tensor", None),
        P(("groups", "job"), "tensor", None),
        P(("groups", "job"), "tensor", None),
        P(("groups", "job"), None),
        P(("groups", "job"), None),
        P("groups"),
        P("groups"),
    )
    small = mesh.shape["job"] == JOBS and mesh.shape["tensor"] == 4
    return jax.shard_map(
        on_device if small else on_any_device,
        mesh=mesh,
        in_specs=placed,
        out_specs=(
            P(("groups", "job"), None, "tensor"),
            P(("groups", "job"), "tensor", None),
            P(("groups", "job"), "tensor", None),
        ),
        check_vma=False,
    )
```

```python
import functools
import math

import jax
import jax.numpy as jnp
from jax import lax
from jax.experimental import pallas as pl
from jax.experimental.pallas import tpu as pltpu
from jax.sharding import PartitionSpec as P

F32 = jnp.float32
BF16 = jnp.bfloat16
VMEM_LIMIT = 28 * 1024 * 1024
CHUNKS = 5
JOBS = 4
PAIR = [(0, 1), (1, 0), (2, 3), (3, 2)]
MIDDLE = [
    pair
    for t in range(4)
    for pair in ((t * 4 + 1, t * 4 + 2), (t * 4 + 2, t * 4 + 1), (t * 4, (t ^ 1) * 4), (t * 4 + 3, (t ^ 1) * 4 + 3))
]
TENSOR_X = [(0, 2), (2, 0), (1, 3), (3, 1)]
TENSOR_CORE = [(0, 1), (1, 0), (2, 3), (3, 2)]


def params():
    return pltpu.CompilerParams(vmem_limit_bytes=VMEM_LIMIT)


def cost(flops, moved):
    return pl.CostEstimate(flops=flops, bytes_accessed=moved, transcendentals=0)


def whole(shape):
    return pl.BlockSpec(shape, lambda *_: (0,) * len(shape))


def far(value):
    return pltpu.with_memory_space_constraint(value, pltpu.HBM)


def smem():
    return pl.BlockSpec(memory_space=pltpu.SMEM)


def turn_kernel(down_ref, low_ref, high_ref):
    turned = down_ref[...].T
    half = low_ref.shape[0]
    low_ref[...] = turned[:half]
    high_ref[...] = turned[half:]


def turn(down, tile):
    width, rank = down.shape
    half = rank // 2
    out = jax.ShapeDtypeStruct((half, width), down.dtype)
    return pl.pallas_call(
        turn_kernel,
        grid=(width // tile,),
        in_specs=[pl.BlockSpec((tile, rank), lambda i: (i, 0))],
        out_specs=[pl.BlockSpec((half, tile), lambda i: (0, i))] * 2,
        out_shape=[out, out],
        compiler_params=params(),
        cost_estimate=cost(0, 4 * width * rank),
        name="turn_adapter",
    )(down)


class Info:
    def __init__(self, ref):
        self.ref = ref
        self.blocks = (ref.shape[0] - 3 - 2 * JOBS) // 2

    @staticmethod
    def pack(ids, lengths, owners, ranks, place):
        return jnp.concatenate([ids[0], lengths[0], owners, ranks, place])

    def adapter(self, b):
        return self.ref[b]

    def length(self, b):
        return self.ref[self.blocks + b]

    def owner(self, adapter):
        return self.ref[2 * self.blocks + adapter]

    def rank(self, adapter):
        return self.ref[2 * self.blocks + JOBS + adapter]

    def place(self):
        first = 2 * self.blocks + 2 * JOBS
        return self.ref[first], self.ref[first + 1], self.ref[first + 2]


def block_factor(info, b, rows, width):
    adapter = info.adapter(b)
    rank = info.rank(adapter)
    live = lax.broadcasted_iota(jnp.int32, (rows, width), 0) < info.length(b)
    keep = lax.broadcasted_iota(jnp.int32, (rows, width), 1) < rank
    scale = jnp.float32(width) / (2.0 * rank.astype(F32))
    return info.owner(adapter), jnp.where(live & keep, scale, 0.0)


def spread(low, slot):
    half = low.shape[1] // 2
    lanes = lax.broadcasted_iota(jnp.int32, low.shape, 1)
    turned = pltpu.roll(low, half, 1)
    twice = jnp.where(lanes < half, low, turned)
    chunk = jnp.where(lanes < half, 0, 1)
    return jnp.concatenate(
        [
            jnp.where(chunk == slot, twice, 0.0),
            jnp.where(chunk + 2 == slot, twice, 0.0),
            jnp.where(lanes < half, turned, 0.0),
        ],
        axis=1,
    )


def gathered(full, slot, rank):
    half = rank // 2
    odd = lax.rem(slot, 2)
    both = jnp.where(slot >= 2, full[:, rank : 2 * rank], full[:, :rank])
    turned = pltpu.roll(both, half, 1)
    lower = jnp.where(odd == 1, turned, both)
    upper = pltpu.roll(full[:, 2 * rank :], half, 1)
    lanes = lax.broadcasted_iota(jnp.int32, both.shape, 1)
    return jnp.where(lanes < half, lower, upper)


def roles(z, excess):
    inner = (z == 1) | (z == 2)
    mine = jnp.where(z < 2, 1, 2)
    far_in = 3 - mine
    far_out = jnp.where(z < 2, 3, 0)
    top_in, top_far_in = excess == mine, excess == far_in
    spare = CHUNKS - 1
    return [
        jnp.where(
            inner, jnp.where(top_far_in, far_out, spare), jnp.where(top_in | top_far_in, far_out, spare)
        ),
        jnp.where(
            inner,
            jnp.where(top_far_in, spare, far_out),
            jnp.where(top_in, far_in, jnp.where(top_far_in, spare, far_out)),
        ),
        jnp.where(inner | top_in, spare, far_in),
        jnp.bitwise_xor(z, 1),
        far_in,
        z,
        jnp.int32(spare),
    ]


def pull_kernel(norm, info, g0, g1, g2, g3, z_ref, x_up_ref, core_ref, x_ref, *rest):
    u0, u2, (u1, u3) = z_ref, x_up_ref, (core_ref.at[0], core_ref.at[1])
    parts, (wide_ref, up, turned, sums) = rest[:7], rest[7:]
    info = Info(info)
    t, z, excess = info.place()
    quarter, values = g0.shape
    rank = up.shape[2]
    half = rank // 2
    block = x_ref.shape[0] // info.blocks

    @pl.when(pl.program_id(0) == 0)
    def _():
        for q, u in enumerate((u0, u1, u2, u3)):
            start = pl.multiple_of(jnp.bitwise_xor(t, q) * quarter, quarter)
            for d in range(JOBS):
                slot = jnp.bitwise_xor(z, d)
                up[slot, pl.ds(start, quarter), :] = u[d]
        for q, g in enumerate((g0, g1, g2, g3)):
            for j in range(quarter // block):
                b = jnp.bitwise_xor(t, q) * (quarter // block) + j
                slot, factor = block_factor(info, b, block, rank)
                pulled = jnp.dot(g[j * block : (j + 1) * block, :], up[slot], preferred_element_type=F32)
                low = spread((pulled * factor).astype(BF16).astype(F32), slot)
                rows = pl.ds(pl.multiple_of(b * block, block), block)
                wide_ref[rows, :] = low.astype(BF16)
                turned[:, rows] = low.T.astype(BF16)

    sums[...] = (
        jnp.dot(turned[: CHUNKS * half, :], x_ref[...], preferred_element_type=F32) * norm
    ).astype(BF16)
    for part, chunk in zip(parts, roles(z, excess)):
        part[...] = sums[pl.ds(pl.multiple_of(chunk * half, half), half), :]


def pull(info, grads, ups, features, norm, tile):
    rows, width = features.shape
    quarter, values = grads[0].shape
    rank = ups[0].shape[2]
    used = CHUNKS * rank // 2
    return pl.pallas_call(
        functools.partial(pull_kernel, norm),
        grid=(width // tile,),
        in_specs=[smem()]
        + [whole((quarter, values))] * 4
        + [whole((JOBS, quarter, rank))] * 2
        + [whole((2, JOBS, quarter, rank))]
        + [pl.BlockSpec((rows, tile), lambda i: (0, i))],
        out_specs=[pl.BlockSpec((rank // 2, tile), lambda i: (0, i))] * 7 + [whole((rows, 3 * rank))],
        out_shape=[jax.ShapeDtypeStruct((rank // 2, width), BF16)] * 7
        + [jax.ShapeDtypeStruct((rows, 3 * rank), BF16)],
        scratch_shapes=[
            pltpu.VMEM((JOBS, values, rank), BF16),
            pltpu.VMEM((3 * rank, rows), BF16),
            pltpu.VMEM((used, tile), BF16),
        ],
        compiler_params=params(),
        cost_estimate=cost(2 * used * rows * width, 2 * (rows * width + used * width + 2 * rows * values)),
        name="pull_and_part_down",
    )(info, far(grads[0]), *grads[1:], *ups, far(features))


def arrivals(z, excess):
    inner = (z == 1) | (z == 2)
    mine = jnp.where(z < 2, 1, 2)
    outer = jnp.where(z < 2, 0, 3)
    far_in, far_out = 3 - mine, 3 - outer
    top_in, top_out = excess == mine, excess == outer
    top_far_in, top_far_out = excess == far_in, excess == far_out
    spare, none = CHUNKS - 1, CHUNKS + 1
    return [
        z,
        jnp.where(excess == z, spare, none),
        jnp.where(inner, outer, mine),
        jnp.where(inner, jnp.where(top_out, spare, none), jnp.where(top_in, spare, far_in)),
        jnp.where(inner, none, jnp.where(top_in, far_in, jnp.where(top_far_in, spare, far_out))),
        jnp.where(
            inner, none, jnp.where(top_in | top_far_in, far_out, jnp.where(top_far_out, spare, none))
        ),
        jnp.where(inner, far_in, none),
        jnp.where(inner, jnp.where(top_far_in, spare, far_out), none),
        jnp.where(
            inner, jnp.where(top_far_in, far_out, jnp.where(top_far_out, spare, none)), none
        ),
    ]


def project_kernel(info, *refs):
    chunks = refs[:9]
    x_ref, out_ref, table_ref, turned, sems = refs[9:]
    info = Info(info)
    half, width = chunks[0].shape
    rank = 2 * half
    rows = x_ref.shape[0]
    used = CHUNKS * half

    @pl.when(pl.program_id(0) == 0)
    def _():
        _, z, excess = info.place()
        where_to = arrivals(z, excess)

        def chunk_copy(k):
            start = pl.multiple_of(where_to[k] * half, half)
            return pltpu.make_async_copy(chunks[k], table_ref.at[pl.ds(start, half), :], sems.at[k])

        for k in range(9):
            pl.when(where_to[k] < CHUNKS)(lambda k=k: chunk_copy(k).start())
        table_ref[used:, :] = jnp.zeros((half, width), BF16)
        for k in range(9):
            pl.when(where_to[k] < CHUNKS)(lambda k=k: chunk_copy(k).wait())

    turned[...] = lax.dot_general(
        table_ref[:used, :], x_ref[...], (((1,), (1,)), ((), ())), preferred_element_type=F32
    )
    first = pl.program_id(0) * (rows // rank)
    for j in range(rows // rank):
        slot = info.owner(info.adapter(first + j))
        columns = slice(j * rank, (j + 1) * rank)
        piece = jnp.concatenate(
            [turned[pl.ds(pl.multiple_of(slot * half, half), half), columns], turned[used - half :, columns]], axis=0
        )
        out_ref[columns, :] = piece.T.astype(BF16)


def project(info, chunks, features, tile):
    rows, width = features.shape
    half = chunks[0].shape[0]
    return pl.pallas_call(
        project_kernel,
        grid=(rows // tile,),
        in_specs=[smem()]
        + [pl.BlockSpec(memory_space=pl.ANY)] * 9
        + [pl.BlockSpec((tile, width), lambda i: (i, 0))],
        out_specs=[
            pl.BlockSpec((tile, 2 * half), lambda i: (i, 0)),
            whole((6 * half, width)),
        ],
        out_shape=[
            jax.ShapeDtypeStruct((rows, 2 * half), BF16),
            jax.ShapeDtypeStruct((6 * half, width), BF16),
        ],
        scratch_shapes=[pltpu.VMEM((CHUNKS * half, tile), F32), pltpu.SemaphoreType.DMA((9,))],
        compiler_params=params(),
        cost_estimate=cost(2 * 6 * half * rows * width, 2 * (rows * width + 12 * half * width)),
        name="project",
    )(info, *chunks, far(features))


def base_kernel(info, g0, g1, g2, g3, weight_ref, out_ref):
    info = Info(info)
    t, _, _ = info.place()
    quarter, values = g0.shape
    block = out_ref.shape[0] // info.blocks
    tile = out_ref.shape[1]
    for q, g in enumerate((g0, g1, g2, g3)):
        start = pl.multiple_of(jnp.bitwise_xor(t, q) * quarter, quarter)
        term = lax.dot_general(
            g[...], weight_ref[...], (((1,), (1,)), ((), ())), preferred_element_type=F32
        )
        for j in range(quarter // block):
            b = jnp.bitwise_xor(t, q) * (quarter // block) + j
            live = lax.broadcasted_iota(jnp.int32, (block, tile), 0) < info.length(b)
            out_ref[pl.ds(pl.multiple_of(start + j * block, block), block), :] = jnp.where(
                live, term[j * block : (j + 1) * block], 0.0
            ).astype(BF16)


def base(info, grads, weight, half_index, tile):
    width, values = weight.shape[0] // 2, weight.shape[1]
    quarter = grads[0].shape[0]
    rows = 4 * quarter
    first = half_index * (width // tile)
    return pl.pallas_call(
        base_kernel,
        grid=(width // tile,),
        in_specs=[smem()]
        + [whole((quarter, values))] * 4
        + [pl.BlockSpec((tile, values), lambda i: (first + i, 0))],
        out_specs=pl.BlockSpec((rows, tile), lambda i: (0, i)),
        out_shape=jax.ShapeDtypeStruct((rows, width), BF16),
        compiler_params=params(),
        cost_estimate=cost(2 * rows * width * values, 2 * (rows * values + width * values + rows * width)),
        name="base_term",
    )(info, *map(far, grads), far(weight))


def rows_kernel(wide_ref, table_ref, base_ref, out_ref):
    out_ref[...] = (
        base_ref[...].astype(F32) + jnp.dot(wide_ref[...], table_ref[...], preferred_element_type=F32)
    ).astype(BF16)


def add_rows(wide, table, base_half, tile):
    rows, deep = wide.shape
    width = table.shape[1]
    return pl.pallas_call(
        rows_kernel,
        grid=(width // tile // 2,),
        in_specs=[
            whole((rows, deep)),
            pl.BlockSpec((deep, tile), lambda i: (0, i)),
            pl.BlockSpec((rows, tile), lambda i: (0, i)),
        ],
        out_specs=pl.BlockSpec((rows, tile), lambda i: (0, i)),
        out_shape=jax.ShapeDtypeStruct((rows, width), BF16),
        compiler_params=params(),
        cost_estimate=cost(rows * width * deep, 2 * (rows * width + deep * (rows + width // 2))),
        name="grad_rows",
    )(wide, table, base_half)


def part_up_kernel(norm, info, g0, g1, g2, g3, a_ref, b_ref, *rest):
    outs, (slice_ref, wide) = rest[:JOBS], rest[JOBS:]
    info = Info(info)
    t, z, excess = info.place()
    quarter, values = g0.shape
    rank = a_ref.shape[1]
    half = rank // 2
    block = a_ref.shape[0] // info.blocks
    columns = pl.ds(pl.multiple_of(t * quarter, quarter), quarter)
    for q, g in enumerate((g0, g1, g2, g3)):
        start = pl.multiple_of(jnp.bitwise_xor(t, q) * quarter, quarter)
        slice_ref[pl.ds(start, quarter), :] = g[:, columns]
    for b in range(info.blocks):
        slot, factor = block_factor(info, b, block, rank)
        rows = slice(b * block, (b + 1) * block)
        low = (a_ref[rows, :].astype(F32) + b_ref[rows, :].astype(F32)) * factor
        wide[rows, :] = spread(low.astype(BF16).astype(F32), slot).astype(BF16)
    full = (
        lax.dot_general(slice_ref[...], wide[...], (((0,), (0,)), ((), ())), preferred_element_type=F32) * norm
    )
    lanes = lax.broadcasted_iota(jnp.int32, (quarter, rank), 1)
    for d, out in enumerate(outs):
        slot = jnp.bitwise_xor(z, d)
        keep = jnp.where(slot == excess, rank, half)
        out[...] = jnp.where(lanes < keep, gathered(full, slot, rank), 0.0).astype(BF16)


def part_up(info, grads, sums, norm):
    quarter, values = grads[0].shape
    rows, rank = sums[0].shape
    vmem = pl.BlockSpec(memory_space=pltpu.VMEM)
    return pl.pallas_call(
        functools.partial(part_up_kernel, norm),
        in_specs=[smem()] + [vmem] * 6,
        out_specs=[vmem] * JOBS,
        out_shape=[jax.ShapeDtypeStruct((quarter, rank), BF16)] * JOBS,
        scratch_shapes=[
            pltpu.VMEM((rows, quarter), BF16),
            pltpu.VMEM((rows, 3 * rank), BF16),
        ],
        compiler_params=params(),
        cost_estimate=cost(2 * rows * quarter * 3 * rank, 2 * (rows * values + 2 * rows * rank)),
        name="part_up",
    )(info, *grads, *sums)


def last_kernel(info, wide_ref, table_ref, base_ref, own0, own1, t1, n1, t2, n2, filled_ref, rows_ref, down_ref):
    del filled_ref
    _, z, excess = Info(info).place()
    half = own0.shape[0]
    rank = 2 * half
    total = (
        jnp.concatenate([own0[...], own1[...]], axis=0).astype(F32)
        + jnp.concatenate([t1[...], t2[...]], axis=0).astype(F32)
    )
    inner = (z == 1) | (z == 2)
    total += jnp.where(inner, jnp.concatenate([n1[...], n2[...]], axis=0).astype(F32), 0.0)
    keep = jnp.where(z == excess, rank, half)
    rows = lax.broadcasted_iota(jnp.int32, total.shape, 0)
    down_ref[...] = jnp.where(rows < keep, total, 0.0).T
    rows_ref[...] = (
        base_ref[...].astype(F32) + jnp.dot(wide_ref[...], table_ref[...], preferred_element_type=F32)
    ).astype(BF16)


def last(info, wide, table, base_half, filled, sums, steps):
    rows, deep = wide.shape
    half, width = sums[0].shape
    tile, piece = width // 2 // steps, width // steps
    return pl.pallas_call(
        last_kernel,
        grid=(steps,),
        in_specs=[
            smem(),
            whole((rows, deep)),
            pl.BlockSpec((deep, tile), lambda i: (0, steps + i)),
            pl.BlockSpec((rows, tile), lambda i: (0, i)),
        ]
        + [pl.BlockSpec((half, piece), lambda i: (0, i))] * 6
        + [pl.BlockSpec(memory_space=pl.ANY)],
        out_specs=[
            pl.BlockSpec((rows, tile), lambda i: (0, steps + i)),
            pl.BlockSpec((piece, 2 * half), lambda i: (i, 0)),
        ],
        out_shape=[
            jax.ShapeDtypeStruct((rows, width), BF16),
            jax.ShapeDtypeStruct((width, 2 * half), F32),
        ],
        input_output_aliases={10: 0},
        compiler_params=params(),
        cost_estimate=cost(rows * width * deep, 2 * (rows * width + deep * (rows + width // 2) + 10 * half * width)),
        name="grad_rows_and_down",
    )(info, wide, table, base_half, *sums, filled)


def on_device(
    inputs,
    grad_out,
    value_weight,
    adapter_down,
    adapter_up,
    block_adapter,
    block_length,
    owner_slot,
    adapter_rank,
):
    features = inputs[0]
    row_count, local_width = features.shape
    half = adapter_down.shape[2] // 2
    tile = 512
    norm = 1.0 / math.sqrt(JOBS * row_count)
    t, z = lax.axis_index("tensor"), lax.axis_index("job")
    excess = jnp.sum(jnp.where(adapter_rank > half, owner_slot, 0)).astype(jnp.int32)
    place = jnp.stack([t, z, excess]).astype(jnp.int32)
    info = Info.pack(block_adapter, block_length, owner_slot, adapter_rank, place)

    inner = (z == 1) | (z == 2)
    mine = jnp.where(z < 2, 1, 2)
    top_in = excess == mine

    pair = lambda value: lax.ppermute(value, "job", PAIR)
    middle = lambda value: lax.ppermute(value, ("tensor", "job"), MIDDLE)
    swap = lambda value, d: lax.ppermute(value, "job", [(i, i ^ d) for i in range(JOBS)])
    across = lambda value: lax.ppermute(value, "tensor", TENSOR_X)
    beside = lambda value: lax.ppermute(value, "tensor", TENSOR_CORE)

    tie = lax.optimization_barrier

    up = adapter_up[0]
    g0 = grad_out[0]
    g2 = across(g0)
    g1 = beside(g0)
    up_z = jnp.stack([up] + [swap(up, d) for d in (1, 2, 3)])
    up_x = across(up_z)

    low, high = turn(adapter_down[0], local_width)
    s1 = pair(low)
    m1 = middle(low)

    up_x, g2, g1, up_z = tie((up_x, g2, g1, up_z))
    to_c = jnp.stack([up_z, up_x])
    s1, m1, to_c, info = tie((s1, m1, to_c, info))
    to_s2 = jnp.where(inner & ~top_in, m1, high)
    to_m2 = jnp.where(top_in, high, s1)
    to_s2, to_m2, to_c, g2 = tie((to_s2, to_m2, to_c, g2))
    s2 = pair(to_s2)
    m2 = middle(to_m2)
    g3 = beside(g2)
    up_c = beside(to_c)

    to_s2, to_m2, up_c, g3 = tie((to_s2, to_m2, up_c, g3))
    grads = (g0, g1, g2, g3)
    ups = (up_z, up_x, up_c)
    *parts, wide = pull(info, grads, ups, features, norm, 1024)

    def added(part, value, use=None):
        value = value.astype(F32)
        return (part.astype(F32) + (value if use is None else jnp.where(use, value, 0.0))).astype(BF16)

    *parts, s2, m2 = tie((*parts, s2, m2))
    to_s3 = jnp.where(inner, jnp.where(top_in, m1, m2), parts[0])
    to_m3 = jnp.where(top_in, s1, s2)
    to_s3, to_m3, *grads = tie((to_s3, to_m3, *grads))
    s3 = pair(to_s3)
    m3 = middle(to_m3)
    base_a = base(info, grads, value_weight, 0, 768)
    s3, m3, base_a = tie((s3, m3, base_a))
    to_s4 = jnp.where(inner, jnp.where(top_in, m2, m3), parts[1])
    to_n3 = added(parts[0], s3, ~top_in)
    to_s4, to_n3, *grads = tie((to_s4, to_n3, *grads))
    s4 = pair(to_s4)
    n3 = middle(to_n3)
    base_b = base(info, grads, value_weight, 1, 768)
    s4, n3, base_b = tie((s4, n3, base_b))

    to_s5 = added(parts[2], n3, inner & ~top_in)
    to_n2 = added(parts[1], jnp.where(top_in, s3, s4))
    to_s5, to_n2, to_project = tie((to_s5, to_n2, s4))
    s5 = pair(to_s5)
    n2 = middle(to_n2)
    partial, table = project(
        info, (low, high, s1, s2, s3, to_project, m1, m2, m3), features, 512
    )
    partial, s5 = tie((partial, s5))
    beyond = across(partial)
    to_s6 = added(parts[3], jnp.where(top_in, n3, n2), inner)
    to_n1 = added(parts[4], jnp.where(top_in, s4, s5))
    to_s6, to_n1, wide, table, base_a, base_b = tie((to_s6, to_n1, wide, table, base_a, base_b))
    s6 = pair(to_s6)
    n1 = middle(to_n1)
    grad_rows = add_rows(wide, table, base_a, 768)
    grad_rows, beyond = tie((grad_rows, beyond))
    both = (partial.astype(F32) + beyond.astype(F32)).astype(BF16)
    other = beside(both)

    ours = part_up(info, grads, (both, other), norm)
    theirs = [swap(ours[d], d) for d in (1, 2, 3)]
    wide, table, base_b, _ = tie((wide, table, base_b, ours[1]))
    grad_rows, grad_down = last(info, wide, table, base_b, grad_rows, (parts[5], parts[6], s6, n1, s5, n2), 4)
    grad_rows, grad_down, *theirs = tie((grad_rows, grad_down, *theirs))
    grad_up = ours[0].astype(F32)
    for value in theirs:
        grad_up = grad_up + value.astype(F32)
    return (grad_rows[None], grad_down[None], grad_up[None])


def block_tables(block_ids, block_sizes, owner_slot, adapter_rank, block_rows, rank_width):
    adapter_count = owner_slot.shape[0]
    matches = (block_ids[:, None] == jnp.arange(adapter_count, dtype=jnp.int32)[None, :]).astype(
        jnp.int32
    )
    slot_index = jnp.sum(matches * owner_slot[None, :], axis=1)
    rank_used = jnp.sum(matches * adapter_rank[None, :], axis=1)
    selector = (slot_index[:, None] == jnp.arange(adapter_count, dtype=jnp.int32)[None, :]).astype(F32)
    live_rows = (jnp.arange(block_rows, dtype=jnp.int32)[None, :] < block_sizes[:, None]).astype(F32)
    keep_ranks = (jnp.arange(rank_width, dtype=jnp.int32)[None, :] < rank_used[:, None]).astype(F32)
    scaling = rank_width / (2.0 * rank_used.astype(F32))
    factor = live_rows[:, :, None] * keep_ranks[:, None, :] * scaling[:, None, None]
    return (slot_index, selector, live_rows, factor)


def on_any_device(
    inputs,
    grad_out,
    value_weight,
    adapter_down,
    adapter_up,
    block_adapter,
    block_length,
    owner_slot,
    adapter_rank,
):
    highest = lax.Precision.HIGHEST
    features = inputs[0]
    row_count, local_width = features.shape
    block_count = block_adapter.shape[1]
    block_rows = row_count // block_count
    rank_width = adapter_down.shape[2]
    local_values = adapter_up.shape[1]
    norm = 1.0 / math.sqrt(lax.axis_size("job") * row_count)
    cotangent = lax.all_gather(grad_out, "tensor", axis=1, tiled=True)[0]
    slot_index, selector, live_rows, factor = block_tables(
        block_adapter[0], block_length[0], owner_slot, adapter_rank, block_rows, rank_width
    )
    base_term = lax.dot_general(
        cotangent, value_weight, (((1,), (1,)), ((), ())), preferred_element_type=F32
    )
    value_start = lax.axis_index("tensor") * local_values
    cot_slice = lax.dynamic_slice_in_dim(cotangent, value_start, local_values, 1).reshape(
        block_count, block_rows, local_values
    )
    feat_blocks = features.reshape(block_count, block_rows, local_width)
    down_all = lax.all_gather(adapter_down, "job", axis=0, tiled=True)
    up_all = lax.all_gather(adapter_up, "job", axis=0, tiled=True)
    down_used = jnp.take(down_all, slot_index, axis=0)
    up_used = jnp.take(up_all, slot_index, axis=0)
    projected = jnp.einsum("btd,bdr->btr", feat_blocks, down_used, preferred_element_type=F32)
    pulled = jnp.einsum("btk,bkr->btr", cot_slice, up_used, preferred_element_type=F32)
    projected = lax.psum(projected.astype(BF16), "tensor").astype(F32)
    pulled = lax.psum(pulled.astype(BF16), "tensor").astype(F32)
    low_down = (projected * factor).astype(BF16)
    low_grad = (pulled * factor).astype(BF16)
    adapter_term = jnp.einsum(
        "btr,bdr->btd", low_grad, down_used, preferred_element_type=F32
    ).reshape(row_count, local_width)
    grad_rows = (base_term * live_rows.reshape(row_count)[:, None] + adapter_term).astype(BF16)[None]
    block_down = jnp.einsum("btd,btr->bdr", feat_blocks, low_grad, preferred_element_type=F32)
    block_up = jnp.einsum("btk,btr->bkr", cot_slice, low_down, preferred_element_type=F32)
    part_down = jnp.einsum("bs,bdr->sdr", selector, block_down, precision=highest) * norm
    part_up_sum = jnp.einsum("bs,bkr->skr", selector, block_up, precision=highest) * norm
    grad_down = lax.psum_scatter(part_down.astype(BF16), "job", scatter_dimension=0, tiled=True).astype(F32)
    grad_up = lax.psum_scatter(part_up_sum.astype(BF16), "job", scatter_dimension=0, tiled=True).astype(F32)
    return (grad_rows, grad_down, grad_up)


def solution(mesh):
    placed = (
        P(("groups", "job"), None, "tensor"),
        P(("groups", "job"), "tensor", None),
        P("tensor", None),
        P(("groups", "job"), "tensor", None),
        P(("groups", "job"), "tensor", None),
        P(("groups", "job"), None),
        P(("groups", "job"), None),
        P("groups"),
        P("groups"),
    )
    small = mesh.shape["job"] == JOBS and mesh.shape["tensor"] == 4
    return jax.shard_map(
        on_device if small else on_any_device,
        mesh=mesh,
        in_specs=placed,
        out_specs=(
            P(("groups", "job"), None, "tensor"),
            P(("groups", "job"), "tensor", None),
            P(("groups", "job"), "tensor", None),
        ),
        check_vma=False,
    )
```
